128 devices in a mesh: les: 4 (over x_lo, core), blk: 32 (over y, x_hi, z).
Axes of the slice: x: 4 (x_hi: 2, x_lo: 2; x = x_hi * 2 + x_lo), y: 4, z: 4, core: 2. Of those that a mesh axis runs over, the one named last changes fastest.
Arguments:
- field_state: float32 [256, 5, 40, 1600], P(('les', 'blk')), may hold values from -6 to 6
- mean_velocity: float32 [256, 3, 40, 1600], P(('les', 'blk')), may hold values from -0.5 to 0.5
- mean_thermo: float32 [256, 2, 40, 1600], P(('les', 'blk')), may hold values from 0.5 to 2
- grid_metric: float32 [256, 3, 40, 1600], P(('les', 'blk')), may hold values from 0.5 to 1.5
- inlet_rows: float32 [2, 8192, 200], P(None, ('les', 'blk')), may hold values from -24 to 24
- row_owner: int32 [8192], P(('les', 'blk')), may hold values from 0 to 10239, as said below
- face_link: int32 [256, 6, 3], P(('les', 'blk')), may hold values from 0 to 255, as said below
- face_kind: int32 [256, 6], P(('les', 'blk')), may hold values from 0 to 2
Outputs:
- section_one: float32 [256, 5, 40, 1600], P(('les', 'blk'))
- section_two: float32 [256, 5, 40, 1600], P(('les', 'blk'))
The draws below stay inside these ranges and needn't reach their ends.
Inputs may be any that keep to these rules, and one draw needn't show every extreme that they name: `row_owner`: among the 64 rows of one device, at most 2 name lines of the blocks of any one device. `face_link`: where face_kind is 0, the partner block lies on the same device or on the device one step along blk (wrapping, same les index); links are mutual, the partner's code being the inverse turn; at most 4 faces of one device link to one neighbouring device. Where face_kind is not 0 the entry names the face itself with code 0.
All inputs are finite; a program needn't handle non-finite values.
Results may differ from the reference program's by a relative error of at most 0.000057.
Values sent between devices are 32-bit elements; how exact they have to be, the bound alone decides.
No kernel may reach another device: no remote copies, remote signals or barrier semaphores. Data moves between devices by JAX's collectives and lax.ppermute only.
A program may use at most 128 MiB of HBM per device.

```python
import math
import jax
import jax.numpy as jnp
from jax import lax

C = 40
BLK_DEV = 2
R_DEV = 64
CAP = 2
FACE_CAP = 4
NDEV = 128
NBLK = 256
ROWS = 8192
NLINES = 10240
NHOT = 16
N_BLK = 32


def inverse_turn(codes):
    flip_first = codes % 2
    flip_second = codes // 2 % 2
    return jnp.where(codes >= 4, 4 + flip_first * 2 + flip_second, codes)


def link_tables(key):
    key = jax.random.fold_in(key, 101)
    key_perm, key_up, key_inner, key_kind = jax.random.split(key, 4)
    faces = 6 * BLK_DEV
    orders = jax.vmap(lambda part_key: jax.random.permutation(part_key, faces))(jax.random.split(key_perm, NDEV))
    devices = jnp.arange(NDEV)
    row_start = devices // N_BLK * N_BLK
    column = devices % N_BLK
    upward = row_start + (column + 1) % N_BLK
    downward = row_start + (column + N_BLK - 1) % N_BLK
    turns_up = jax.random.randint(key_up, (NDEV, FACE_CAP), 0, 8)
    turns_inner = jax.random.randint(key_inner, (NDEV,), 0, 8)
    rest = faces - 2 * FACE_CAP - 2
    rest_kinds = jax.random.randint(key_kind, (NDEV, rest), 1, 3)
    owner_rows = jnp.broadcast_to(devices[:, None], (NDEV, FACE_CAP))
    partner_device = jnp.zeros((NDEV, faces), jnp.int32)
    partner_face = jnp.zeros((NDEV, faces), jnp.int32)
    partner_turn = jnp.zeros((NDEV, faces), jnp.int32)
    kinds = jnp.zeros((NDEV, faces), jnp.int32)
    up_faces = orders[:, :FACE_CAP]
    partner_device = partner_device.at[owner_rows, up_faces].set(jnp.broadcast_to(upward[:, None], (NDEV, FACE_CAP)))
    partner_face = partner_face.at[owner_rows, up_faces].set(orders[upward][:, FACE_CAP:2 * FACE_CAP])
    partner_turn = partner_turn.at[owner_rows, up_faces].set(turns_up)
    down_faces = orders[:, FACE_CAP:2 * FACE_CAP]
    partner_device = partner_device.at[owner_rows, down_faces].set(jnp.broadcast_to(downward[:, None], (NDEV, FACE_CAP)))
    partner_face = partner_face.at[owner_rows, down_faces].set(orders[downward][:, :FACE_CAP])
    partner_turn = partner_turn.at[owner_rows, down_faces].set(inverse_turn(turns_up[downward]))
    inner_first = orders[:, 2 * FACE_CAP]
    inner_second = orders[:, 2 * FACE_CAP + 1]
    partner_device = partner_device.at[devices, inner_first].set(devices)
    partner_device = partner_device.at[devices, inner_second].set(devices)
    partner_face = partner_face.at[devices, inner_first].set(inner_second)
    partner_face = partner_face.at[devices, inner_second].set(inner_first)
    partner_turn = partner_turn.at[devices, inner_first].set(turns_inner)
    partner_turn = partner_turn.at[devices, inner_second].set(inverse_turn(turns_inner))
    rest_faces = orders[:, 2 * FACE_CAP + 2:]
    rest_rows = jnp.broadcast_to(devices[:, None], (NDEV, rest))
    partner_device = partner_device.at[rest_rows, rest_faces].set(rest_rows)
    partner_face = partner_face.at[rest_rows, rest_faces].set(rest_faces)
    partner_turn = partner_turn.at[rest_rows, rest_faces].set(0)
    kinds = kinds.at[rest_rows, rest_faces].set(rest_kinds)
    block = partner_device * BLK_DEV + partner_face // 6
    links = jnp.stack([block, partner_face % 6, partner_turn], axis=-1)
    return (links.reshape(NBLK, 6, 3).astype(jnp.int32), kinds.reshape(NBLK, 6).astype(jnp.int32))


def draw_face_link(key, part):
    tables = link_tables(key)
    return tables[0]


def draw_face_kind(key, part):
    tables = link_tables(key)
    return tables[1]


def draw_field_state(key, part):
    key = jax.random.fold_in(key, 23)
    key_rough = jax.random.fold_in(key, 0)
    shape = (NBLK, 5, C, C * C)
    return jax.random.truncated_normal(key_rough, -6.0, 6.0, shape, jnp.float32)


def draw_row_owner(key, part):
    key = jax.random.fold_in(key, 7)
    key_order, key_rows = jax.random.split(key)
    ranking = jax.random.permutation(key_order, NDEV)
    busy = ranking[:NHOT]
    quiet = ranking[NHOT:]
    half = R_DEV // 2
    lines = BLK_DEV * C

    def one_device(device_key):
        key_busy, key_quiet, key_shuffle, key_line = jax.random.split(device_key, 4)
        busy_slots = jax.random.permutation(key_busy, NHOT * CAP)[:half]
        quiet_slots = jax.random.permutation(key_quiet, (NDEV - NHOT) * CAP)[:R_DEV - half]
        target = jnp.concatenate([busy[busy_slots // CAP], quiet[quiet_slots // CAP]])
        target = target[jax.random.permutation(key_shuffle, R_DEV)]
        local_line = jax.random.randint(key_line, (R_DEV,), 0, lines)
        return target * lines + local_line
    owners = jax.vmap(one_device)(jax.random.split(key_rows, NDEV))
    return owners.reshape(-1).astype(jnp.int32)


def shard_levels(rng, dims, cuts, low, largest):
    loudness, own = 1.0, jax.random.fold_in(rng, 6)
    for axis_at, parts in cuts:
        steps = jnp.exp(jax.random.uniform(jax.random.fold_in(own, axis_at), (parts,), jnp.float32, low / len(cuts), largest / len(cuts)))
        loudness = loudness * jnp.repeat(steps, dims[axis_at] // parts).reshape([-1 if axis == axis_at else 1 for axis in range(len(dims))])
    return loudness


def bell_draw(own_key, extent, scale, limit, cuts=(), held_as=jnp.bfloat16):
    values = jax.random.normal(own_key, extent, jnp.float32) * scale
    if len(cuts) > 0:
        values = shard_levels(own_key, extent, cuts, -0.22, 0.18) * values
    return jnp.clip(values, min=-limit, max=limit).astype(held_as)


def setup_inputs(seed: int = 0) -> dict:
    arg_keys = jax.random.split(jax.random.key(seed), 9)
    return {
        "field_state": draw_field_state(jax.random.fold_in(arg_keys[8], 71), 0),
        "mean_velocity": jnp.clip(jax.random.uniform(arg_keys[1], (NBLK, 3, C, C * C), jnp.float32, -0.5, 0.5) * shard_levels(arg_keys[1], (NBLK, 3, C, C * C), ((0, 128),), -0.4, 0.0), -0.5, 0.5),
        "mean_thermo": jnp.clip(jnp.exp(math.log(2.0) - 1.3862944 * jax.random.uniform(arg_keys[2], (NBLK, 2, C, C * C), jnp.float32) ** shard_levels(arg_keys[2], (NBLK, 2, C, C * C), ((0, 128),), -0.2, 0.2)), 0.5, 2.0),
        "grid_metric": jnp.clip(jnp.exp(math.log(1.5) - 1.0986123 * jax.random.uniform(arg_keys[3], (NBLK, 3, C, C * C), jnp.float32) ** shard_levels(arg_keys[3], (NBLK, 3, C, C * C), ((0, 128),), -0.2, 0.2)), 0.5, 1.5),
        "inlet_rows": bell_draw(arg_keys[4], (2, ROWS, 5 * C), 4.0, 24.0, ((1, 128),), jnp.float32),
        "row_owner": draw_row_owner(jax.random.fold_in(arg_keys[8], 71), 0),
        "face_link": draw_face_link(jax.random.fold_in(arg_keys[8], 71), 0),
        "face_kind": draw_face_kind(jax.random.fold_in(arg_keys[8], 71), 0),
    }


COEFFS = (0.75, -0.15, 1.0 / 60.0)
GAMMA_GAS = 1.4
TIME_STEP = 0.5
SECTION_WEIGHTS = (0.117979901, 0.184646966)


def face_layers(volume):
    lower_x = jnp.transpose(volume[:, :, 0:3], (0, 2, 1, 3, 4))
    upper_x = jnp.transpose(volume[:, :, ::-1][:, :, 0:3], (0, 2, 1, 3, 4))
    lower_y = jnp.transpose(volume[:, :, :, 0:3], (0, 3, 1, 2, 4))
    upper_y = jnp.transpose(volume[:, :, :, ::-1][:, :, :, 0:3], (0, 3, 1, 2, 4))
    lower_z = jnp.transpose(volume[..., 0:3], (0, 4, 1, 2, 3))
    upper_z = jnp.transpose(volume[..., ::-1][..., 0:3], (0, 4, 1, 2, 3))
    return jnp.stack([lower_x, upper_x, lower_y, upper_y, lower_z, upper_z], axis=1)


def turn_faces(faces, codes):
    codes = codes[:, None, None, None, None]
    faces = jnp.where(codes >= 4, jnp.swapaxes(faces, -1, -2), faces)
    faces = jnp.where(codes % 2 == 1, jnp.flip(faces, -2), faces)
    return jnp.where((codes // 2) % 2 == 1, jnp.flip(faces, -1), faces)


def fill_ghosts(own_faces, arrived, kinds):
    kinds = kinds[:, None, None, None, None]
    return jnp.where(kinds == 0, arrived, jnp.where(kinds == 1, own_faces, jnp.zeros_like(own_faces)))


def central(padded, axis, width):
    def window(start):
        return lax.slice_in_dim(padded, start, start + width, axis=axis)
    return (COEFFS[0] * (window(4) - window(2)) + COEFFS[1] * (window(5) - window(1))
            + COEFFS[2] * (window(6) - window(0)))


def rates(volume, ghosts, velocity, thermo, metric, source):
    width = volume.shape[2]

    def lower(layers, order):
        return jnp.transpose(layers[:, ::-1], order)

    def upper(layers, order):
        return jnp.transpose(layers, order)

    order_x = (0, 2, 1, 3, 4)
    order_y = (0, 2, 3, 1, 4)
    order_z = (0, 2, 3, 4, 1)
    padded_x = jnp.concatenate([lower(ghosts[:, 0], order_x), volume, upper(ghosts[:, 1], order_x)], axis=2)
    padded_y = jnp.concatenate([lower(ghosts[:, 2], order_y), volume, upper(ghosts[:, 3], order_y)], axis=3)
    padded_z = jnp.concatenate([lower(ghosts[:, 4], order_z), volume, upper(ghosts[:, 5], order_z)], axis=4)
    along_x = metric[:, 0:1] * central(padded_x, 2, width)
    along_y = metric[:, 1:2] * central(padded_y, 3, width)
    along_z = metric[:, 2:3] * central(padded_z, 4, width)
    carried = velocity[:, 0:1] * along_x + velocity[:, 1:2] * along_y + velocity[:, 2:3] * along_z
    spread = along_x[:, 1] + along_y[:, 2] + along_z[:, 3]
    density = thermo[:, 0]
    pressure = thermo[:, 1]
    result = jnp.stack([
        -(carried[:, 0] + density * spread),
        -(carried[:, 1] + along_x[:, 4] / density),
        -(carried[:, 2] + along_y[:, 4] / density),
        -(carried[:, 3] + along_z[:, 4] / density),
        -(carried[:, 4] + GAMMA_GAS * pressure * spread)], axis=1)
    return result.at[:, :, 0].add(source)


def rates_grouped(volume, ghosts, velocity, thermo, metric, source):
    groups = volume.shape[0] // 2

    def regroup(array):
        return array.reshape((groups, 2) + array.shape[1:])

    operands = (regroup(volume), regroup(ghosts), regroup(velocity), regroup(thermo), regroup(metric), regroup(source))
    result = lax.map(lambda pieces: rates(*pieces), operands)
    return result.reshape(volume.shape)


def reference(field_state, mean_velocity, mean_thermo, grid_metric, inlet_rows, row_owner, face_link, face_kind):
    start = field_state.reshape(NBLK, 5, C, C, C)
    velocity = mean_velocity.reshape(NBLK, 3, C, C, C)
    thermo = mean_thermo.reshape(NBLK, 2, C, C, C)
    metric = grid_metric.reshape(NBLK, 3, C, C, C)
    partner = (face_link[:, :, 0] * 6 + face_link[:, :, 1]).reshape(-1).astype(jnp.int32)
    codes = face_link[:, :, 2].reshape(-1)
    kinds = face_kind.reshape(-1)

    def ghosts_of(volume):
        own_faces = face_layers(volume).reshape(NBLK * 6, 3, 5, C, C)
        arrived = turn_faces(own_faces[partner], codes)
        return fill_ghosts(own_faces, arrived, kinds).reshape(NBLK, 6, 3, 5, C, C)

    def source_of(section_rows):
        summed = jax.ops.segment_sum(section_rows, row_owner, num_segments=NLINES)
        return jnp.transpose(summed.reshape(NBLK, C, 5, C), (0, 2, 1, 3))

    first = (TIME_STEP * SECTION_WEIGHTS[0]) * rates_grouped(
        start, ghosts_of(start), velocity, thermo, metric, source_of(inlet_rows[0]))
    middle = start + first
    second = (TIME_STEP * SECTION_WEIGHTS[1]) * rates_grouped(
        middle, ghosts_of(middle), velocity, thermo, metric, source_of(inlet_rows[1]))
    return first.reshape(field_state.shape), second.reshape(field_state.shape)
```

```python
import functools

import jax
import jax.numpy as jnp
import numpy as np
from jax import lax
from jax.experimental import pallas as pl
from jax.experimental.pallas import tpu as pltpu
from jax.sharding import PartitionSpec as P

CAP = 2
FACE_CAP = 4
W = 40
PLANE = W * W
FIELDS = 5
ROWS = FIELDS * W
TILES = 13
INTS = (45.0, -9.0, 1.0)
GAMMA_GAS = 1.4
TIME_STEP = 0.5
SECTION_WEIGHTS = (0.117979901, 0.184646966)
VMEM_LIMIT = 56 * 1024 * 1024
F32 = jnp.float32
BF16 = jnp.bfloat16


def weight_of(offset):
    total = np.zeros(offset.shape, np.float32)
    for step in range(3):
        total += INTS[step] * ((offset == step + 1).astype(np.float32) - (offset == -step - 1))
    return total


def second_table():
    k = np.arange(512)[:, None] - 128
    lane = np.arange(256)[None, :]
    gap = k - lane
    return weight_of(np.where(gap % W == 0, gap // W, 99))


def third_tables():
    tables = []
    for n in range(5):
        k = np.arange(512)[:, None] - 128 + 256 * n
        lane = np.arange(256)[None, :] + 256 * n
        same = (k // W) == (lane // W)
        tables.append(weight_of(np.where(same, k - lane, 99)))
    return np.stack(tables)


def third_ghost_table():
    lane = np.arange(PLANE)[None, :]
    out = np.zeros((256, PLANE), np.float32)
    edge = np.arange(3 * W)[:, None]
    depth, across = edge // W, edge % W
    match = across == lane // W
    out[: 3 * W] = match * weight_of(-1 - depth - lane % W)
    out[128 : 128 + 3 * W] = match * weight_of(W + depth - lane % W)
    return out


def third_pick_table():
    lane = np.arange(PLANE)[:, None]
    out = np.zeros((PLANE, 256), np.float32)
    edge = np.arange(3 * W)[None, :]
    depth, across = edge // W, edge % W
    match = across == lane // W
    out[:, : 3 * W] = match & (lane % W == depth)
    out[:, 128 : 128 + 3 * W] = match & (lane % W == W - 1 - depth)
    return out


def iota(shape, dim):
    return lax.broadcasted_iota(jnp.int32, shape, dim)


def split3(x):
    high = x.astype(BF16)
    rest = x - high.astype(F32)
    mid = rest.astype(BF16)
    low = (rest - mid.astype(F32)).astype(BF16)
    return high, mid, low


def product3(x, table):
    total = None
    for part in split3(x):
        term = jnp.dot(part, table, preferred_element_type=F32)
        total = term if total is None else total + term
    return total


def roll_lanes(x, by):
    by = by % 128
    return x if by == 0 else pltpu.roll(x, by, x.ndim - 1)


def lane_tile(ref, lead, rows, t):
    if t < 12:
        return ref[lead + (rows, pl.ds(128 * t, 128))]
    part = ref[lead + (rows, pl.ds(1536, 64))]
    return jnp.concatenate([part, jnp.zeros(part.shape[:-1] + (64,), F32)], axis=-1)


def combine(dx, dy, dz, velocity, thermo, metric, scale):
    density, pressure = thermo
    carried = [None] * FIELDS
    spread = None
    inverse = 1.0 / density
    extra = {}
    for d, grad in enumerate((dx, dy, dz)):
        if grad is None:
            continue
        m = metric[d] * scale
        a = velocity[d] * m
        for f in range(FIELDS):
            term = a * grad[f]
            carried[f] = term if carried[f] is None else carried[f] + term
        term = m * grad[1 + d]
        spread = term if spread is None else spread + term
        extra[1 + d] = (m * inverse) * grad[4]
    out = [carried[0] + density * spread]
    for f in (1, 2, 3):
        out.append(carried[f] + extra[f] if f in extra else carried[f])
    out.append(carried[4] + (GAMMA_GAS * pressure) * spread)
    return out


def extract(x_ref, pick_ref, own_ref, strips):
    lane = iota((W, 128), 1)
    for f in range(FIELDS):
        rows = pl.ds(f * W, W)
        own_ref[2, rows, :] = x_ref[0, f, :, pl.ds(0, 128)]
        b = lane_tile(x_ref, (0, f), pl.ds(0, W), 11)
        a = lane_tile(x_ref, (0, f), pl.ds(0, W), 12)
        middle = jnp.where(lane < 56, roll_lanes(b, 56), roll_lanes(a, 56))
        own_ref[3, rows, :] = jnp.where(
            lane < 40, roll_lanes(a, -24), jnp.where(lane < 80, middle, roll_lanes(b, 8))
        )
    picked = product3(x_ref[0].reshape(ROWS, PLANE), pick_ref[...])
    own_ref[4] = picked[:, :128]
    own_ref[5] = picked[:, 128:]
    sub = iota((8, 128), 0)
    lane8 = iota((8, 128), 1)
    for t in range(TILES):
        for f in range(FIELDS):
            low = lane_tile(x_ref, (0, f), pl.ds(0, 8), t)
            high = lane_tile(x_ref, (0, f), pl.ds(32, 8), t)
            both = jnp.where(sub < 4, low, high)
            for y in range(W):
                start = W * y - 128 * t
                if start >= 0 and start < 128:
                    value = roll_lanes(both, -start)
                    strips[pl.ds(y * W + f * 8, 8), :] = value
                elif start < 0 and start + W > 0:
                    value = roll_lanes(both, -start)
                    old = strips[pl.ds(y * W + f * 8, 8), :]
                    strips[pl.ds(y * W + f * 8, 8), :] = jnp.where(lane8 < -start, old, value)
    for f in range(FIELDS):
        rows = pl.ds(f * W, W)
        for side in range(2):
            parts = []
            for k in range(3):
                row = f * 8 + (7 - k if side else k)
                parts.append(roll_lanes(strips[pl.ds(row, W, stride=W), :], W * k))
            own_ref[side, rows, :] = jnp.where(
                lane < 40, parts[0], jnp.where(lane < 80, parts[1], parts[2])
            )


def spread_faces(own_ref, up_ref, down_ref, meta_ref, block):
    for face in range(6):
        place = meta_ref[1, block * 6 + face]

        @pl.when((place >= 1) & (place < 1 + FACE_CAP))
        def _():
            up_ref[place - 1] = own_ref[face]

        @pl.when(place >= 1 + FACE_CAP)
        def _():
            down_ref[place - 1 - FACE_CAP] = own_ref[face]


def flatten_strips(strips, write):
    lane = iota((W, 128), 1)
    for t in range(TILES):
        total = None
        for y in range(W):
            start = W * y - 128 * t
            if start + W <= 0 or start >= 128:
                continue
            value = roll_lanes(strips[pl.ds(y * W, W), :], start)
            if total is None:
                total = value
            else:
                total = jnp.where(lane >= start, value, total)
        write(t, total)


def first_kernel(link_ref, kind_ref, x_ref, pick_ref, own_ref, up_ref, down_ref, meta_ref, strips):
    block = pl.program_id(0)
    cycle = lax.axis_size("blk")
    row_start = lax.axis_index("les") * cycle
    column = lax.axis_index("blk")
    above = row_start + lax.rem(column + 1, cycle)
    below = row_start + lax.rem(column + cycle - 1, cycle)

    @pl.when(block == 0)
    def _():
        partner, from_below, from_above = [], [], []
        ups = jnp.int32(0)
        downs = jnp.int32(0)
        for i in range(12):
            target = link_ref[i // 6, i % 6, 0]
            device = lax.shift_right_logical(target, 1)
            linked = kind_ref[i // 6, i % 6] == 0
            local = (target - 2 * device) * 6 + link_ref[i // 6, i % 6, 1]
            is_up = linked & (device == above)
            is_down = linked & (device == below)
            partner.append(local)
            from_above.append(is_up)
            from_below.append(is_down)
            place = jnp.where(is_up, 1 + ups, jnp.where(is_down, 1 + FACE_CAP + downs, 0))
            meta_ref[1, i] = place
            ups = ups + is_up.astype(jnp.int32)
            downs = downs + is_down.astype(jnp.int32)
        for i in range(12):
            below_rank = jnp.int32(0)
            above_rank = jnp.int32(0)
            for j in range(12):
                less = partner[j] < partner[i]
                below_rank = below_rank + (from_below[j] & less).astype(jnp.int32)
                above_rank = above_rank + (from_above[j] & less).astype(jnp.int32)
            meta_ref[0, i] = jnp.where(
                from_below[i],
                12 + below_rank,
                jnp.where(from_above[i], 12 + FACE_CAP + above_rank, partner[i]),
            )

    extract(x_ref, pick_ref, own_ref, strips)
    spread_faces(own_ref, up_ref, down_ref, meta_ref, block)


def interior_kernel(scale, x_ref, vel_ref, th_ref, me_ref, ty_ref, tz_ref, out_ref, d_ref):
    for n in range(7):
        low = max(0, 256 * n - 128)
        high = min(PLANE, 256 * n + 384)
        skip = low - (256 * n - 128)
        size = high - low
        wide = min(256, PLANE - 256 * n)
        slot = n % 2
        window = x_ref[0, :, :, pl.ds(low, size)].reshape(ROWS, size)
        parts = split3(window)
        for which, table in (
            (0, ty_ref[pl.ds(skip, size), pl.ds(0, wide)]),
            (1, tz_ref[n % 5, pl.ds(skip, size), pl.ds(0, wide)]),
        ):
            total = None
            for part in parts:
                term = jnp.dot(part, table, preferred_element_type=F32)
                total = term if total is None else total + term
            d_ref[slot, which, :, pl.ds(0, wide)] = total
        for at in range(0, wide, 128):
            w = min(128, wide - at)
            lanes = pl.ds(256 * n + at, w)
            sub = iota((8, w), 0)
            for g in range(5):
                rows = pl.ds(8 * g, 8)
                dx, dy, dz = [], [], []
                for f in range(FIELDS):
                    cur = x_ref[0, f, rows, lanes]
                    zero = jnp.zeros_like(cur)
                    before = x_ref[0, f, pl.ds(8 * g - 8, 8), lanes] if g > 0 else zero
                    after = x_ref[0, f, pl.ds(8 * g + 8, 8), lanes] if g < 4 else zero
                    total = None
                    for j in (1, 2, 3):
                        plus = pltpu.roll(jnp.where(sub >= j, cur, after), 8 - j, 0)
                        minus = pltpu.roll(jnp.where(sub < 8 - j, cur, before), j, 0)
                        term = INTS[j - 1] * (plus - minus)
                        total = term if total is None else total + term
                    dx.append(total)
                    dy.append(d_ref[slot, 0, pl.ds(f * W + 8 * g, 8), pl.ds(at, w)])
                    dz.append(d_ref[slot, 1, pl.ds(f * W + 8 * g, 8), pl.ds(at, w)])
                out = combine(
                    dx,
                    dy,
                    dz,
                    [vel_ref[0, d, rows, lanes] for d in range(3)],
                    [th_ref[0, d, rows, lanes] for d in range(2)],
                    [me_ref[0, d, rows, lanes] for d in range(3)],
                    scale,
                )
                for f in range(FIELDS):
                    out_ref[0, f, rows, lanes] = -out[f]


def turn_face(pool, source, code, keep, faces, slot, swapped):
    @pl.when(code >= 4)
    def _():
        lane = iota((W, 128), 1)
        whole = jnp.concatenate([pool[source], jnp.zeros((56, 128), F32)], axis=0)
        left = jnp.transpose(whole[:128])
        right = jnp.transpose(whole[128:])
        for f in range(FIELDS):
            parts = []
            for k in range(3):
                rows = slice(k * W, k * W + W)
                shift = W * k - W * f
                if f < 3:
                    piece = left[rows]
                elif f == 3:
                    piece = jnp.where(lane >= 120, left[rows], right[rows])
                else:
                    piece = right[rows]
                parts.append(roll_lanes(piece, shift))
            swapped[pl.ds(f * W, W), :] = jnp.where(
                lane < 40, parts[0], jnp.where(lane < 80, parts[1], parts[2])
            )

    @pl.when(code < 4)
    def _():
        swapped[...] = pool[source]

    flip_a = code % 2
    flip_b = (code // 2) % 2
    lane = iota((8, 128), 1)
    depth = (lane >= 40).astype(jnp.int32) + (lane >= 80).astype(jnp.int32)
    mirrored = jnp.where(lane < 120, 2 * W * depth + (W - 1) - lane, lane)
    lane_index = jnp.where(flip_b == 1, mirrored, lane)
    sub = iota((8, 128), 0)
    sub_index = jnp.where(flip_a == 1, 7 - sub, sub)
    for f in range(FIELDS):
        for g in range(5):
            start = f * W + 8 * jnp.where(flip_a == 1, 4 - g, g)
            value = swapped[pl.ds(pl.multiple_of(start, 8), 8), :]
            value = jnp.take_along_axis(value, lane_index, axis=1, mode="promise_in_bounds")
            value = jnp.take_along_axis(value, sub_index, axis=0, mode="promise_in_bounds")
            faces[slot, pl.ds(f * W + 8 * g, 8), :] = value * keep


def second_ghosts(face_low, face_high, yg):
    lane = iota((W, 128), 1)

    def near(face):
        first = INTS[0] * face + INTS[1] * roll_lanes(face, -40) + INTS[2] * roll_lanes(face, -80)
        second = INTS[1] * roll_lanes(face, 40) + INTS[2] * face
        third = INTS[2] * roll_lanes(face, 80)
        return jnp.where(
            lane < 40,
            first,
            jnp.where(lane < 80, second, jnp.where(lane < 120, third, jnp.zeros_like(face))),
        )

    for f in range(FIELDS):
        rows = pl.ds(f * W, W)
        yg[0, rows, :] = -near(face_low(rows))
        value = near(face_high(rows))
        crossing = roll_lanes(value, -56)
        zero = jnp.zeros_like(value)
        yg[1, rows, :] = jnp.where(
            lane >= 112, crossing, jnp.where(lane >= 72, roll_lanes(value, -8), zero)
        )
        yg[2, rows, :] = jnp.where(
            lane < 24, crossing, jnp.where(lane < 64, roll_lanes(value, 24), zero)
        )


def finish_kernel(scale, last, *refs):
    refs = list(refs)
    meta_ref, link_ref, kind_ref = refs[:3]
    own_hbm, below_hbm, above_hbm, q_ref, part_ref, vel_ref, th_ref, me_ref, src_ref = refs[3:12]
    zg_table = refs[12]
    if last:
        section_ref = refs[13]
        scratch = refs[14:]
    else:
        pick_ref, section_ref, mid_ref, own_ref, up_ref, down_ref = refs[13:19]
        scratch = refs[19:]
    pool, faces, swapped, strips, yg, zg, flat, sems = scratch
    block = pl.program_id(0)

    @pl.when(block == 0)
    def _():
        copies = [
            pltpu.make_async_copy(own_hbm, pool.at[pl.ds(0, 12)], sems.at[0]),
            pltpu.make_async_copy(below_hbm, pool.at[pl.ds(12, FACE_CAP)], sems.at[1]),
            pltpu.make_async_copy(above_hbm, pool.at[pl.ds(12 + FACE_CAP, FACE_CAP)], sems.at[2]),
        ]
        for copy in copies:
            copy.start()
        for copy in copies:
            copy.wait()

    for face in range(6):
        keep = jnp.where(kind_ref[block, face] == 2, 0.0, 1.0).astype(F32)
        turn_face(
            pool,
            meta_ref[0, block * 6 + face],
            link_ref[block, face, 2],
            keep,
            faces,
            face,
            swapped.at[face],
        )

    both = jnp.concatenate([faces[4], faces[5]], axis=1)
    zg[...] = product3(both, zg_table[...])
    second_ghosts(lambda rows: faces[2, rows, :], lambda rows: faces[3, rows, :], yg)
    for f in range(FIELDS):
        for side in range(2):
            value = faces[side, pl.ds(f * W, W), :]
            for k in range(3):
                row = f * 8 + (7 - k if side else k)
                strips[pl.ds(row, W, stride=W), :] = roll_lanes(value, -W * k)

    def write(t, value):
        flat[:, pl.ds(128 * t, 128)] = value

    flatten_strips(strips, write)

    for t in range(TILES):
        w = 128 if t < 12 else 64
        lanes = pl.ds(128 * t, w)
        sub = iota((8, w), 0)
        for g in range(5):
            rows = pl.ds(8 * g, 8)
            dx = dy = None
            if g in (0, 4):
                dx = []
                for f in range(FIELDS):
                    ghost = [
                        flat[pl.ds(f * 8 + (7 - k if g else k), 1), lanes] for k in range(3)
                    ]
                    far = (7 - sub) if g else sub
                    total = jnp.zeros((8, w), F32)
                    for m in range(3):
                        row = None
                        for k in range(3 - m):
                            term = INTS[m + k] * ghost[k]
                            row = term if row is None else row + term
                        total = jnp.where(far == m, row, total)
                    dx.append(total if g else -total)
            if t in (0, 11, 12):
                spot = {0: 0, 11: 1, 12: 2}[t]
                dy = [yg[spot, pl.ds(f * W + 8 * g, 8), pl.ds(0, w)] for f in range(FIELDS)]
            dz = [zg[pl.ds(f * W + 8 * g, 8), lanes] for f in range(FIELDS)]
            out = combine(
                dx,
                dy,
                dz,
                [vel_ref[0, d, rows, lanes] for d in range(3)],
                [th_ref[0, d, rows, lanes] for d in range(2)],
                [me_ref[0, d, rows, lanes] for d in range(3)],
                scale / 60.0,
            )
            for f in range(FIELDS):
                value = part_ref[0, f, rows, lanes] - out[f]
                if g == 0:
                    line = scale * src_ref[0, 0, pl.ds(f, 1), lanes]
                    value = jnp.where(sub == 0, value + line, value)
                section_ref[0, f, rows, lanes] = value
                if not last:
                    mid_ref[0, f, rows, lanes] = q_ref[0, f, rows, lanes] + value

    if not last:
        extract(mid_ref, pick_ref, own_ref, strips)
        spread_faces(own_ref, up_ref, down_ref, meta_ref, block)


def pack_kernel(owner_ref, rows_ref, out_ref, count, wide):
    devices = out_ref.shape[0]
    rows = owner_ref.shape[0]
    sub = iota((8, 128), 0)
    lane = iota((8, 128), 1)
    empty = jnp.where((sub % 4 == 1) & (lane == 127), -1.0, 0.0).astype(F32)
    wide[...] = jnp.zeros_like(wide)
    for s in range(2):
        wide[2 * s] = rows_ref[s, :, pl.ds(0, 128)]
        wide[2 * s + 1, :, pl.ds(0, 72)] = rows_ref[s, :, pl.ds(128, 72)]

    def clear(d, carry):
        count[d] = 0
        out_ref[d] = empty
        return carry

    lax.fori_loop(0, devices, clear, 0)
    lane1 = iota((1, 128), 1)

    def place(i, carry):
        line = owner_ref[i]
        target = line // (2 * W)
        local = (line - target * (2 * W)).astype(F32)
        slot = count[target]
        count[target] = slot + 1
        for s in range(2):
            for j in range(2):
                value = wide[2 * s + j, pl.ds(i, 1), :]
                if s == 0 and j == 1:
                    value = jnp.where(lane1 == 127, local, value)
                out_ref[target, pl.ds(4 * slot + 2 * s + j, 1), :] = value
        return carry

    lax.fori_loop(0, rows, place, 0)


def inject_kernel(got_ref, out_ref, strips):
    rows = got_ref.shape[0] // 4
    lane = iota((rows, 128), 1)
    parts = [got_ref[pl.ds(j, rows, stride=4), :] for j in range(4)]
    label = jnp.max(jnp.where(lane == 127, parts[1], -1.0), axis=1, keepdims=True)
    chosen = jnp.where(label == lane.astype(F32), 1.0, 0.0)
    chooser = jnp.transpose(chosen).astype(BF16)
    lane = iota((W, 128), 1)
    for s in range(2):
        sums = []
        for j in range(2):
            total = None
            for part in split3(parts[2 * s + j]):
                term = jnp.dot(chooser, part, preferred_element_type=F32)
                total = term if total is None else total + term
            sums.append(total)
        for b in range(2):
            left, right = (value[b * W : b * W + W] for value in sums)
            for f in range(FIELDS):
                if f < 3:
                    piece = left
                elif f == 3:
                    piece = jnp.where(lane >= 120, left, right)
                else:
                    piece = right
                strips[pl.ds(f, W, stride=8), :] = roll_lanes(piece, -W * f)
            lane8 = iota((8, 128), 1)
            for t in range(TILES):
                total = None
                for y in range(W):
                    start = W * y - 128 * t
                    if start + W <= 0 or start >= 128:
                        continue
                    value = roll_lanes(strips[pl.ds(y * 8, 8), :], start)
                    total = value if total is None else jnp.where(lane8 >= start, value, total)
                out_ref[s, b, :, pl.ds(128 * t, 128)] = total


def whole(shape):
    return pl.BlockSpec(shape, lambda b, n=len(shape): (0,) * n)


def per_block(shape):
    return pl.BlockSpec((1,) + shape, lambda b, n=len(shape): (b,) + (0,) * n)


SMEM = pl.BlockSpec(memory_space=pltpu.SMEM)
ANY = pl.BlockSpec(memory_space=pl.ANY)


def params():
    return pltpu.CompilerParams(vmem_limit_bytes=VMEM_LIMIT)


def cost(flops, size):
    return pl.CostEstimate(flops=flops, bytes_accessed=size, transcendentals=0)


VOLUME = (FIELDS, W, PLANE)
FACE = (ROWS, 128)
FACE_OUT = [
    jax.ShapeDtypeStruct((12,) + FACE, F32),
    jax.ShapeDtypeStruct((FACE_CAP,) + FACE, F32),
    jax.ShapeDtypeStruct((FACE_CAP,) + FACE, F32),
]
FACE_SPECS = [
    pl.BlockSpec((6,) + FACE, lambda b: (b, 0, 0)),
    whole((FACE_CAP,) + FACE),
    whole((FACE_CAP,) + FACE),
]


def first_faces(face_link, face_kind, field, pick):
    return pl.pallas_call(
        first_kernel,
        grid=(2,),
        in_specs=[SMEM, SMEM, per_block(VOLUME), whole((PLANE, 256))],
        out_specs=FACE_SPECS + [SMEM],
        out_shape=FACE_OUT + [jax.ShapeDtypeStruct((2, 12), jnp.int32)],
        scratch_shapes=[pltpu.VMEM((W * W, 128), F32)],
        compiler_params=params(),
        cost_estimate=cost(10**9, 6 * 10**6),
        name="first_faces",
    )(face_link, face_kind, field, pick)


def interior(scale, field, velocity, thermo, metric, ty, tz):
    return pl.pallas_call(
        functools.partial(interior_kernel, scale / 60.0),
        grid=(2,),
        in_specs=[
            per_block(VOLUME),
            per_block((3, W, PLANE)),
            per_block((2, W, PLANE)),
            per_block((3, W, PLANE)),
            whole((512, 256)),
            whole((5, 512, 256)),
        ],
        out_specs=per_block(VOLUME),
        out_shape=jax.ShapeDtypeStruct((2,) + VOLUME, F32),
        scratch_shapes=[pltpu.VMEM((2, 2, ROWS, 256), F32)],
        compiler_params=params(),
        cost_estimate=cost(6 * 10**9, 12 * 10**6),
        name="interior",
    )(field, velocity, thermo, metric, ty, tz)


def finish(scale, section, last, meta, link, kind, own, below, above, q, part, vel, th, me, src, zg, pick):
    in_specs = [
        SMEM,
        SMEM,
        SMEM,
        ANY,
        ANY,
        ANY,
        per_block(VOLUME),
        per_block(VOLUME),
        per_block((3, W, PLANE)),
        per_block((2, W, PLANE)),
        per_block((3, W, PLANE)),
        pl.BlockSpec((1, 1, 8, 128 * TILES), lambda b: (section, b, 0, 0)),
        whole((256, PLANE)),
    ]
    operands = [meta, link, kind, own, below, above, q, part, vel, th, me, src, zg]
    volume = jax.ShapeDtypeStruct((2,) + VOLUME, F32)
    out_specs = [per_block(VOLUME)]
    out_shape = [volume]
    if not last:
        in_specs.append(whole((PLANE, 256)))
        operands.append(pick)
        out_specs += [per_block(VOLUME)] + FACE_SPECS
        out_shape += [volume] + FACE_OUT
    return pl.pallas_call(
        functools.partial(finish_kernel, scale, last),
        grid=(2,),
        in_specs=in_specs,
        out_specs=out_specs,
        out_shape=out_shape,
        scratch_shapes=[
            pltpu.VMEM((12 + 2 * FACE_CAP,) + FACE, F32),
            pltpu.VMEM((6,) + FACE, F32),
            pltpu.VMEM((6,) + FACE, F32),
            pltpu.VMEM((W * W, 128), F32),
            pltpu.VMEM((3,) + FACE, F32),
            pltpu.VMEM((ROWS, PLANE), F32),
            pltpu.VMEM((W, 128 * TILES), F32),
            pltpu.SemaphoreType.DMA((3,)),
        ],
        compiler_params=params(),
        cost_estimate=cost(2 * 10**9, 16 * 10**6),
        name="finish_last" if last else "finish_first",
    )(*operands)


def pack(owner, rows, devices):
    vmem = pl.BlockSpec(memory_space=pltpu.VMEM)
    return pl.pallas_call(
        pack_kernel,
        in_specs=[SMEM, vmem],
        out_specs=vmem,
        out_shape=jax.ShapeDtypeStruct((devices, 8, 128), F32),
        scratch_shapes=[pltpu.SMEM((devices,), jnp.int32), pltpu.VMEM((4, rows.shape[1], 128), F32)],
        compiler_params=params(),
        name="pack_rows",
    )(owner, rows)


def inject(got):
    vmem = pl.BlockSpec(memory_space=pltpu.VMEM)
    return pl.pallas_call(
        inject_kernel,
        in_specs=[vmem],
        out_specs=vmem,
        out_shape=jax.ShapeDtypeStruct((2, 2, 8, 128 * TILES), F32),
        scratch_shapes=[pltpu.VMEM((W * 8, 128), F32)],
        compiler_params=params(),
        name="inject_rows",
    )(got)


def shifted(x, by):
    n = lax.axis_size("blk")
    return lax.ppermute(x, "blk", [(i, (i + by) % n) for i in range(n)])


def local(field, velocity, thermo, metric, inlet_rows, row_owner, face_link, face_kind):
    devices = lax.axis_size("les") * lax.axis_size("blk")
    ty = jnp.asarray(second_table(), BF16)
    tz = jnp.asarray(third_tables(), BF16)
    zg = jnp.asarray(third_ghost_table(), BF16)
    pick = jnp.asarray(third_pick_table(), BF16)
    c1, c2 = (TIME_STEP * w for w in SECTION_WEIGHTS)

    own, up, down, meta = first_faces(face_link, face_kind, field, pick)
    below, above = shifted(up, 1), shifted(down, -1)
    sent = pack(row_owner, inlet_rows, devices)
    got = lax.all_to_all(sent, ("les", "blk"), split_axis=0, concat_axis=0, tiled=True)
    src = inject(got.reshape(devices * 8, 128))
    part = interior(c1, field, velocity, thermo, metric, ty, tz)
    first, middle, own, up, down = finish(
        c1, 0, False, meta, face_link, face_kind, own, below, above, field, part,
        velocity, thermo, metric, src, zg, pick,
    )
    below, above = shifted(up, 1), shifted(down, -1)
    part = interior(c2, middle, velocity, thermo, metric, ty, tz)
    (second,) = finish(
        c2, 1, True, meta, face_link, face_kind, own, below, above, middle, part,
        velocity, thermo, metric, src, zg, pick,
    )
    return first, second


def solution(mesh):
    both = ("les", "blk")
    return jax.shard_map(
        local,
        mesh=mesh,
        in_specs=(
            P(both, None, None, None),
            P(both, None, None, None),
            P(both, None, None, None),
            P(both, None, None, None),
            P(None, both, None),
            P(both),
            P(both, None, None),
            P(both, None),
        ),
        out_specs=(P(both, None, None, None), P(both, None, None, None)),
        check_vma=False,
    )
```

```python
import functools

import jax
import jax.numpy as jnp
import numpy as np
from jax import lax
from jax.experimental import pallas as pl
from jax.experimental.pallas import tpu as pltpu
from jax.sharding import PartitionSpec as P

CAP = 2
FACE_CAP = 4
W = 40
PLANE = W * W
FIELDS = 5
ROWS = FIELDS * W
TILES = 13
INTS = (45.0, -9.0, 1.0)
GAMMA_GAS = 1.4
TIME_STEP = 0.5
SECTION_WEIGHTS = (0.117979901, 0.184646966)
VMEM_LIMIT = 28 * 1024 * 1024
F32 = jnp.float32
BF16 = jnp.bfloat16


def weight_of(offset):
    total = np.zeros(offset.shape, np.float32)
    for step in range(3):
        total += INTS[step] * ((offset == step + 1).astype(np.float32) - (offset == -step - 1))
    return total


def second_table():
    k = np.arange(512)[:, None] - 128
    lane = np.arange(256)[None, :]
    gap = k - lane
    return weight_of(np.where(gap % W == 0, gap // W, 99))


def third_tables():
    tables = []
    for n in range(5):
        k = np.arange(512)[:, None] - 128 + 256 * n
        lane = np.arange(256)[None, :] + 256 * n
        same = (k // W) == (lane // W)
        tables.append(weight_of(np.where(same, k - lane, 99)))
    return np.stack(tables)


def third_ghost_table():
    lane = np.arange(PLANE)[None, :]
    out = np.zeros((256, PLANE), np.float32)
    edge = np.arange(3 * W)[:, None]
    depth, across = edge // W, edge % W
    match = across == lane // W
    out[: 3 * W] = match * weight_of(-1 - depth - lane % W)
    out[128 : 128 + 3 * W] = match * weight_of(W + depth - lane % W)
    return out


def third_pick_table():
    lane = np.arange(PLANE)[:, None]
    out = np.zeros((PLANE, 256), np.float32)
    edge = np.arange(3 * W)[None, :]
    depth, across = edge // W, edge % W
    match = across == lane // W
    out[:, : 3 * W] = match & (lane % W == depth)
    out[:, 128 : 128 + 3 * W] = match & (lane % W == W - 1 - depth)
    return out


def iota(shape, dim):
    return lax.broadcasted_iota(jnp.int32, shape, dim)


def split3(x):
    high = x.astype(BF16)
    rest = x - high.astype(F32)
    mid = rest.astype(BF16)
    low = (rest - mid.astype(F32)).astype(BF16)
    return high, mid, low


def product3(x, table):
    total = None
    for part in split3(x):
        term = jnp.dot(part, table, preferred_element_type=F32)
        total = term if total is None else total + term
    return total


def roll_lanes(x, by):
    by = by % 128
    return x if by == 0 else pltpu.roll(x, by, x.ndim - 1)


def lane_tile(ref, lead, rows, t):
    if t < 12:
        return ref[lead + (rows, pl.ds(128 * t, 128))]
    part = ref[lead + (rows, pl.ds(1536, 64))]
    return jnp.concatenate([part, jnp.zeros(part.shape[:-1] + (64,), F32)], axis=-1)


def combine(dx, dy, dz, velocity, thermo, metric, scale):
    density, pressure = thermo
    carried = [None] * FIELDS
    spread = None
    inverse = 1.0 / density
    extra = {}
    for d, grad in enumerate((dx, dy, dz)):
        if grad is None:
            continue
        m = metric[d] * scale
        a = velocity[d] * m
        for f in range(FIELDS):
            term = a * grad[f]
            carried[f] = term if carried[f] is None else carried[f] + term
        term = m * grad[1 + d]
        spread = term if spread is None else spread + term
        extra[1 + d] = (m * inverse) * grad[4]
    out = [carried[0] + density * spread]
    for f in (1, 2, 3):
        out.append(carried[f] + extra[f] if f in extra else carried[f])
    out.append(carried[4] + (GAMMA_GAS * pressure) * spread)
    return out


def extract(x_ref, block, pick_ref, own_ref, strips):
    base = 6 * block
    lane = iota((W, 128), 1)
    for f in range(FIELDS):
        rows = pl.ds(f * W, W)
        own_ref[base + 2, rows, :] = x_ref[block, f, :, pl.ds(0, 128)]
        b = lane_tile(x_ref, (block, f), pl.ds(0, W), 11)
        a = lane_tile(x_ref, (block, f), pl.ds(0, W), 12)
        middle = jnp.where(lane < 56, roll_lanes(b, 56), roll_lanes(a, 56))
        own_ref[base + 3, rows, :] = jnp.where(
            lane < 40, roll_lanes(a, -24), jnp.where(lane < 80, middle, roll_lanes(b, 8))
        )
    picked = product3(x_ref[block].reshape(ROWS, PLANE), pick_ref[...])
    own_ref[base + 4] = picked[:, :128]
    own_ref[base + 5] = picked[:, 128:]
    sub = iota((8, 128), 0)
    lane8 = iota((8, 128), 1)
    for t in range(TILES):
        for f in range(FIELDS):
            low = lane_tile(x_ref, (block, f), pl.ds(0, 8), t)
            high = lane_tile(x_ref, (block, f), pl.ds(32, 8), t)
            both = jnp.where(sub < 4, low, high)
            for y in range(W):
                start = W * y - 128 * t
                if start >= 0 and start < 128:
                    value = roll_lanes(both, -start)
                    strips[pl.ds(y * W + f * 8, 8), :] = value
                elif start < 0 and start + W > 0:
                    value = roll_lanes(both, -start)
                    old = strips[pl.ds(y * W + f * 8, 8), :]
                    strips[pl.ds(y * W + f * 8, 8), :] = jnp.where(lane8 < -start, old, value)
    for f in range(FIELDS):
        rows = pl.ds(f * W, W)
        for side in range(2):
            parts = []
            for k in range(3):
                row = f * 8 + (7 - k if side else k)
                parts.append(roll_lanes(strips[pl.ds(row, W, stride=W), :], W * k))
            own_ref[base + side, rows, :] = jnp.where(
                lane < 40, parts[0], jnp.where(lane < 80, parts[1], parts[2])
            )


def hand_out(own_ref, a_ref, b_ref, meta_ref):
    for face in range(12):
        place = meta_ref[1, face]

        @pl.when((place >= 1) & (place < 1 + FACE_CAP))
        def _():
            a_ref[place - 1] = own_ref[face]

        @pl.when(place >= 1 + FACE_CAP)
        def _():
            b_ref[place - 1 - FACE_CAP] = own_ref[face]


def flatten_strips(strips, write):
    lane = iota((W, 128), 1)
    for t in range(TILES):
        total = None
        for y in range(W):
            start = W * y - 128 * t
            if start + W <= 0 or start >= 128:
                continue
            value = roll_lanes(strips[pl.ds(y * W, W), :], start)
            if total is None:
                total = value
            else:
                total = jnp.where(lane >= start, value, total)
        write(t, total)


def second_ghosts(face_low, face_high, yg):
    lane = iota((W, 128), 1)

    def near(face):
        first = INTS[0] * face + INTS[1] * roll_lanes(face, -40) + INTS[2] * roll_lanes(face, -80)
        second = INTS[1] * roll_lanes(face, 40) + INTS[2] * face
        third = INTS[2] * roll_lanes(face, 80)
        return jnp.where(
            lane < 40,
            first,
            jnp.where(lane < 80, second, jnp.where(lane < 120, third, jnp.zeros_like(face))),
        )

    for f in range(FIELDS):
        rows = pl.ds(f * W, W)
        yg[0, rows, :] = -near(face_low(rows))
        value = near(face_high(rows))
        crossing = roll_lanes(value, -56)
        zero = jnp.zeros_like(value)
        yg[1, rows, :] = jnp.where(
            lane >= 112, crossing, jnp.where(lane >= 72, roll_lanes(value, -8), zero)
        )
        yg[2, rows, :] = jnp.where(
            lane < 24, crossing, jnp.where(lane < 64, roll_lanes(value, 24), zero)
        )


def turn_face(own_ref, a_ref, b_ref, source, code, keep, faces, slot, swapped):
    @pl.when(source < 12)
    def _():
        swapped[...] = own_ref[source]

    @pl.when((source >= 12) & (source < 12 + FACE_CAP))
    def _():
        swapped[...] = a_ref[source - 12]

    @pl.when(source >= 12 + FACE_CAP)
    def _():
        swapped[...] = b_ref[source - 12 - FACE_CAP]

    @pl.when(code >= 4)
    def _():
        lane = iota((W, 128), 1)
        whole = jnp.concatenate([swapped[...], jnp.zeros((56, 128), F32)], axis=0)
        left = jnp.transpose(whole[:128])
        right = jnp.transpose(whole[128:])
        for f in range(FIELDS):
            parts = []
            for k in range(3):
                rows = slice(k * W, k * W + W)
                shift = W * k - W * f
                if f < 3:
                    piece = left[rows]
                elif f == 3:
                    piece = jnp.where(lane >= 120, left[rows], right[rows])
                else:
                    piece = right[rows]
                parts.append(roll_lanes(piece, shift))
            swapped[pl.ds(f * W, W), :] = jnp.where(
                lane < 40, parts[0], jnp.where(lane < 80, parts[1], parts[2])
            )

    flip_a = code % 2
    flip_b = (code // 2) % 2
    lane = iota((8, 128), 1)
    depth = (lane >= 40).astype(jnp.int32) + (lane >= 80).astype(jnp.int32)
    mirrored = jnp.where(lane < 120, 2 * W * depth + (W - 1) - lane, lane)
    lane_index = jnp.where(flip_b == 1, mirrored, lane)
    sub = iota((8, 128), 0)
    sub_index = jnp.where(flip_a == 1, 7 - sub, sub)
    for f in range(FIELDS):
        for g in range(5):
            start = f * W + 8 * jnp.where(flip_a == 1, 4 - g, g)
            value = swapped[pl.ds(pl.multiple_of(start, 8), 8), :]
            value = jnp.take_along_axis(value, lane_index, axis=1, mode="promise_in_bounds")
            value = jnp.take_along_axis(value, sub_index, axis=0, mode="promise_in_bounds")
            faces[slot, pl.ds(f * W + 8 * g, 8), :] = value * keep


def prepare_ghosts(block, meta_ref, link_ref, kind_ref, own_ref, a_ref, b_ref, scratch):
    faces, swapped, strips, yg, flat = scratch
    for face in range(6):
        keep = jnp.where(kind_ref[block, face] == 2, 0.0, 1.0).astype(F32)
        turn_face(
            own_ref,
            a_ref,
            b_ref,
            meta_ref[0, block * 6 + face],
            link_ref[2, block, face],
            keep,
            faces,
            face,
            swapped.at[face],
        )
    second_ghosts(lambda rows: faces[2, rows, :], lambda rows: faces[3, rows, :], yg)
    for f in range(FIELDS):
        for side in range(2):
            value = faces[side, pl.ds(f * W, W), :]
            for k in range(3):
                row = f * 8 + (7 - k if side else k)
                strips[pl.ds(row, W, stride=W), :] = roll_lanes(value, -W * k)

    def write(t, value):
        flat[:, pl.ds(128 * t, 128)] = value

    flatten_strips(strips, write)


GHOST_SCRATCH = [
    pltpu.VMEM((6, ROWS, 128), F32),
    pltpu.VMEM((6, ROWS, 128), F32),
    pltpu.VMEM((W * W, 128), F32),
    pltpu.VMEM((3, ROWS, 128), F32),
    pltpu.VMEM((W, 128 * TILES), F32),
]


def add(a, b):
    return b if a is None else a + b


def inner_first(x_ref, block, f, g, lanes, w):
    sub = iota((8, w), 0)
    cur = x_ref[block, f, pl.ds(8 * g, 8), lanes]
    zero = jnp.zeros_like(cur)
    before = x_ref[block, f, pl.ds(8 * g - 8, 8), lanes] if g > 0 else zero
    after = x_ref[block, f, pl.ds(8 * g + 8, 8), lanes] if g < 4 else zero
    total = None
    for j in (1, 2, 3):
        plus = pltpu.roll(jnp.where(sub >= j, cur, after), 8 - j, 0)
        minus = pltpu.roll(jnp.where(sub < 8 - j, cur, before), j, 0)
        total = add(total, INTS[j - 1] * (plus - minus))
    return total


def ghost_first(flat, f, g, lanes, w):
    sub = iota((8, w), 0)
    ghost = [flat[pl.ds(f * 8 + (7 - k if g else k), 1), lanes] for k in range(3)]
    far = (7 - sub) if g else sub
    total = jnp.zeros((8, w), F32)
    for m in range(3):
        row = None
        for k in range(3 - m):
            row = add(row, INTS[m + k] * ghost[k])
        total = jnp.where(far == m, row, total)
    return total if g else -total


def sweep(block, scale, x_ref, tables, ghosts, means, d_ref, emit):
    vel_ref, th_ref, me_ref = means
    if ghosts is not None:
        faces, _, _, yg, flat, zg_ref = ghosts
        edge = split3(jnp.concatenate([faces[4], faces[5]], axis=1))
    for n in range(7):
        wide = min(256, PLANE - 256 * n)
        slot = n % 2
        along = [None, None]
        if x_ref is not None:
            ty_ref, tz_ref = tables
            low = max(0, 256 * n - 128)
            high = min(PLANE, 256 * n + 384)
            skip = low - (256 * n - 128)
            size = high - low
            parts = split3(x_ref[block, :, :, pl.ds(low, size)].reshape(ROWS, size))
            ty = ty_ref[pl.ds(skip, size), pl.ds(0, wide)]
            tz = tz_ref[n % 5, pl.ds(skip, size), pl.ds(0, wide)]
            for part in parts:
                along[0] = add(along[0], jnp.dot(part, ty, preferred_element_type=F32))
                along[1] = add(along[1], jnp.dot(part, tz, preferred_element_type=F32))
        if ghosts is not None:
            table = zg_ref[:, pl.ds(256 * n, wide)]
            for part in edge:
                along[1] = add(along[1], jnp.dot(part, table, preferred_element_type=F32))
        for which in range(2):
            if along[which] is not None:
                d_ref[slot, which, :, pl.ds(0, wide)] = along[which]
        for at in range(0, wide, 128):
            w = min(128, wide - at)
            t = 2 * n + at // 128
            lanes = pl.ds(128 * t, w)
            for g in range(5):
                rows = pl.ds(8 * g, 8)
                dx, dy, dz = [], [], []
                for f in range(FIELDS):
                    own_rows = pl.ds(f * W + 8 * g, 8)
                    x = y = None
                    if x_ref is not None:
                        x = inner_first(x_ref, block, f, g, lanes, w)
                        y = d_ref[slot, 0, own_rows, pl.ds(at, w)]
                    if ghosts is not None:
                        if g in (0, 4):
                            x = add(x, ghost_first(flat, f, g, lanes, w))
                        if t in (0, 11, 12):
                            y = add(y, yg[{0: 0, 11: 1, 12: 2}[t], own_rows, pl.ds(0, w)])
                    dx.append(x)
                    dy.append(y)
                    dz.append(d_ref[slot, 1, own_rows, pl.ds(at, w)])
                out = combine(
                    dx if dx[0] is not None else None,
                    dy if dy[0] is not None else None,
                    dz,
                    [vel_ref[block, d, rows, lanes] for d in range(3)],
                    [th_ref[block, d, rows, lanes] for d in range(2)],
                    [me_ref[block, d, rows, lanes] for d in range(3)],
                    scale / 60.0,
                )
                for f in range(FIELDS):
                    emit(f, g, rows, lanes, w, out[f])


def both_blocks(body):
    def step(block, carry):
        body(block)
        return carry

    lax.fori_loop(0, 2, step, 0)


def pack(owner_ref, rows_ref, out_ref, count, wide):
    devices = out_ref.shape[0]
    rows = owner_ref.shape[0]
    sub = iota((8, 128), 0)
    lane = iota((8, 128), 1)
    empty = jnp.where((sub % 4 == 1) & (lane == 127), -1.0, 0.0).astype(F32)
    wide[...] = jnp.zeros_like(wide)
    for s in range(2):
        wide[2 * s] = rows_ref[s, :, pl.ds(0, 128)]
        wide[2 * s + 1, :, pl.ds(0, 72)] = rows_ref[s, :, pl.ds(128, 72)]

    def clear(d, carry):
        count[d] = 0
        out_ref[d] = empty
        return carry

    lax.fori_loop(0, devices, clear, 0, unroll=8)
    lane1 = iota((1, 128), 1)

    def place(i, carry):
        line = owner_ref[i]
        target = lax.shift_right_logical(line * 52429, 22)
        local = (line - target * (2 * W)).astype(F32)
        slot = count[target]
        count[target] = slot + 1
        for s in range(2):
            for j in range(2):
                value = wide[2 * s + j, pl.ds(i, 1), :]
                if s == 0 and j == 1:
                    value = jnp.where(lane1 == 127, local, value)
                out_ref[target, pl.ds(4 * slot + 2 * s + j, 1), :] = value
        return carry

    lax.fori_loop(0, rows, place, 0, unroll=8)


def first_kernel(
    owner_hbm,
    rows_hbm,
    link_hbm,
    kind_hbm,
    x_hbm,
    pick_hbm,
    sent_hbm,
    own_hbm,
    a_hbm,
    b_hbm,
    meta_hbm,
    owner_ref,
    count,
    link_ref,
    kind_ref,
    meta_ref,
    rows_ref,
    wide,
    sent,
    x_ref,
    pick_ref,
    own_ref,
    strips,
    sems,
    own_sems,
    hand_sems,
):
    loads = [
        pltpu.make_async_copy(*pair, sems.at[i])
        for i, pair in enumerate(
            [
                (owner_hbm, owner_ref),
                (rows_hbm, rows_ref),
                (link_hbm, link_ref),
                (kind_hbm, kind_ref),
                (pick_hbm, pick_ref),
                (x_hbm.at[0], x_ref.at[0]),
                (x_hbm.at[1], x_ref.at[1]),
            ]
        )
    ]
    for load in loads:
        load.start()
    for load in loads[:4]:
        load.wait()
    pack(owner_ref, rows_ref, sent, count, wide)
    send = pltpu.make_async_copy(sent, sent_hbm, sems.at[7])
    send.start()
    cycle = lax.axis_size("blk")
    row_start = lax.axis_index("les") * cycle
    column = lax.axis_index("blk")
    above = row_start + lax.rem(column + 1, cycle)
    below = row_start + lax.rem(column + cycle - 1, cycle)
    even = lax.rem(column, 2) == 0
    partner_a = jnp.where(even, above, below)
    partner_b = jnp.where(even, below, above)
    partner, to_a, to_b = [], [], []
    count_a = jnp.int32(0)
    count_b = jnp.int32(0)
    for i in range(12):
        target = link_ref[0, i // 6, i % 6]
        device = lax.shift_right_logical(target, 1)
        linked = kind_ref[i // 6, i % 6] == 0
        is_a = linked & (device == partner_a)
        is_b = linked & (device == partner_b)
        partner.append((target - 2 * device) * 6 + link_ref[1, i // 6, i % 6])
        to_a.append(is_a)
        to_b.append(is_b)
        meta_ref[1, i] = jnp.where(is_a, 1 + count_a, jnp.where(is_b, 1 + FACE_CAP + count_b, 0))
        count_a = count_a + is_a.astype(jnp.int32)
        count_b = count_b + is_b.astype(jnp.int32)
    for i in range(12):
        rank_a = jnp.int32(0)
        rank_b = jnp.int32(0)
        for j in range(12):
            less = partner[j] < partner[i]
            rank_a = rank_a + (to_a[j] & less).astype(jnp.int32)
            rank_b = rank_b + (to_b[j] & less).astype(jnp.int32)
        meta_ref[0, i] = jnp.where(
            to_a[i], 12 + rank_a, jnp.where(to_b[i], 12 + FACE_CAP + rank_b, partner[i])
        )
    meta_out = pltpu.make_async_copy(meta_ref, meta_hbm, sems.at[8])
    meta_out.start()
    for load in loads[4:]:
        load.wait()

    def copies(face):
        place = meta_ref[1, face]
        return (
            (place >= 1) & (place < 1 + FACE_CAP),
            lambda: pltpu.make_async_copy(
                own_ref.at[face], a_hbm.at[place - 1], hand_sems.at[face]
            ),
            place >= 1 + FACE_CAP,
            lambda: pltpu.make_async_copy(
                own_ref.at[face], b_hbm.at[place - 1 - FACE_CAP], hand_sems.at[face]
            ),
        )

    def keep(block):
        return pltpu.make_async_copy(
            own_ref.at[pl.ds(6 * block, 6)], own_hbm.at[pl.ds(6 * block, 6)], own_sems.at[block]
        )

    def body(block):
        extract(x_ref, block, pick_ref, own_ref, strips)
        for i in range(6):
            is_a, copy_a, is_b, copy_b = copies(6 * block + i)

            @pl.when(is_a)
            def _():
                copy_a().start()

            @pl.when(is_b)
            def _():
                copy_b().start()

        keep(block).start()

    both_blocks(body)
    for face in range(12):
        is_a, copy_a, is_b, copy_b = copies(face)

        @pl.when(is_a)
        def _():
            copy_a().wait()

        @pl.when(is_b)
        def _():
            copy_b().wait()

    for block in range(2):
        keep(block).wait()
    send.wait()
    meta_out.wait()


def load_all(pairs, sems):
    loads = [pltpu.make_async_copy(*pair, sems.at[i]) for i, pair in enumerate(pairs)]
    for load in loads:
        load.start()
    return loads


def section_kernel(scale, *refs):
    sources, out_hbm = refs[:13], refs[13]
    held, out = refs[14:27], refs[27]
    ghost, d_ref, sems, out_sems = refs[28:33], refs[33], refs[34], refs[35]
    loads = load_all(zip(sources, held), sems)
    meta, link, kind, own, a, b, zg, ty, tz, x_ref, vel, th, me = held
    for load in loads[:6]:
        load.wait()

    def store(block):
        return pltpu.make_async_copy(out.at[block], out_hbm.at[block], out_sems.at[block])

    def body(block):
        prepare_ghosts(block, meta, link, kind, own, a, b, ghost)

        @pl.when(block == 0)
        def _():
            for load in loads[6:]:
                load.wait()

        def emit(f, g, rows, lanes, w, value):
            out[block, f, rows, lanes] = -value

        sweep(block, scale, x_ref, (ty, tz), tuple(ghost) + (zg,), (vel, th, me), d_ref, emit)
        store(block).start()

    both_blocks(body)
    for block in range(2):
        store(block).wait()


def inject(got_ref, src, strips):
    rows = got_ref.shape[0] // 4
    lane = iota((rows, 128), 1)
    parts = [got_ref[pl.ds(j, rows, stride=4), :] for j in range(4)]
    label = jnp.max(jnp.where(lane == 127, parts[1], -1.0), axis=1, keepdims=True)
    chosen = jnp.where(label == lane.astype(F32), 1.0, 0.0)
    chooser = jnp.transpose(chosen).astype(BF16)
    lane = iota((W, 128), 1)
    lane8 = iota((8, 128), 1)
    for s in range(2):
        sums = []
        for j in range(2):
            total = None
            for part in split3(parts[2 * s + j]):
                total = add(total, jnp.dot(chooser, part, preferred_element_type=F32))
            sums.append(total)
        for b in range(2):
            left, right = (value[b * W : b * W + W] for value in sums)
            for f in range(FIELDS):
                if f < 3:
                    piece = left
                elif f == 3:
                    piece = jnp.where(lane >= 120, left, right)
                else:
                    piece = right
                strips[pl.ds(f, W, stride=8), :] = roll_lanes(piece, -W * f)
            for t in range(TILES):
                total = None
                for y in range(W):
                    start = W * y - 128 * t
                    if start + W <= 0 or start >= 128:
                        continue
                    value = roll_lanes(strips[pl.ds(y * 8, 8), :], start)
                    total = value if total is None else jnp.where(lane8 >= start, value, total)
                src[s, b, :, pl.ds(128 * t, 128)] = total


def middle_kernel(scale, *refs):
    sources, outs = refs[:5], refs[5:11]
    section, mid, own, a, b, src = outs
    held, strips, lines, sems = refs[11:16], refs[16], refs[17], refs[18]
    loads = load_all(zip(sources, held), sems)
    meta, got, pre, q_ref, pick = held
    loads[0].wait()
    loads[1].wait()
    inject(got, src, lines)
    for load in loads[2:]:
        load.wait()

    def body(block):
        for f in range(FIELDS):
            value = pre[block, f]
            line = scale * src[0, block, pl.ds(f, 1), pl.ds(0, PLANE)]
            top = value[:8]
            top = jnp.where(iota((8, PLANE), 0) == 0, top + line, top)
            section[block, f, pl.ds(0, 8), :] = top
            section[block, f, pl.ds(8, W - 8), :] = value[8:]
            mid[block, f, pl.ds(0, 8), :] = q_ref[block, f, pl.ds(0, 8), :] + top
            mid[block, f, pl.ds(8, W - 8), :] = q_ref[block, f, pl.ds(8, W - 8), :] + value[8:]
        extract(mid, block, pick, own, strips)

    both_blocks(body)
    hand_out(own, a, b, meta)


def interior_kernel(scale, x_ref, section, vel, th, me, ty, tz, part, out_hbm, d_ref, sem):
    copy = pltpu.make_async_copy(section, out_hbm, sem)
    copy.start()

    def body(block):
        def emit(f, g, rows, lanes, w, value):
            part[block, f, rows, lanes] = -value

        sweep(block, scale, x_ref, (ty, tz), None, (vel, th, me), d_ref, emit)

    both_blocks(body)
    copy.wait()


def last_kernel(scale, *refs):
    meta, link, kind, own, a, b, part, vel, th, me, zg, src, out_hbm = refs[:13]
    ghost, d_ref, out, sems = refs[13:18], refs[18], refs[19], refs[20]

    def copy(block):
        return pltpu.make_async_copy(out.at[block], out_hbm.at[block], sems.at[block])

    def body(block):
        prepare_ghosts(block, meta, link, kind, own, a, b, ghost)

        def emit(f, g, rows, lanes, w, value):
            value = part[block, f, rows, lanes] - value
            if g == 0:
                line = scale * src[1, block, pl.ds(f, 1), lanes]
                value = jnp.where(iota((8, w), 0) == 0, value + line, value)
            out[block, f, rows, lanes] = value

        sweep(block, scale, None, None, tuple(ghost) + (zg,), (vel, th, me), d_ref, emit)
        copy(block).start()

    both_blocks(body)
    for block in range(2):
        copy(block).wait()


SMEM = pl.BlockSpec(memory_space=pltpu.SMEM)
VMEM = pl.BlockSpec(memory_space=pltpu.VMEM)
ANY = pl.BlockSpec(memory_space=pl.ANY)


def near(x):
    return pltpu.with_memory_space_constraint(x, pltpu.VMEM)


def far(x):
    return pltpu.with_memory_space_constraint(x, pltpu.HBM)


def cost(flops, size):
    return pl.CostEstimate(flops=flops, bytes_accessed=size, transcendentals=0)


def call(kernel, name, arrays, outs, scratch, flops=0, size=10**6, smem=(), remote=()):
    specs = [VMEM if spot is None else spot for spot, _ in outs]
    return pl.pallas_call(
        kernel,
        in_specs=[SMEM] * len(smem) + [ANY] * len(remote) + [VMEM] * len(arrays),
        out_specs=specs,
        out_shape=[shape for _, shape in outs],
        scratch_shapes=scratch,
        compiler_params=pltpu.CompilerParams(vmem_limit_bytes=VMEM_LIMIT),
        cost_estimate=cost(flops, size),
        name=name,
    )(*smem, *[far(x) for x in remote], *[near(x) for x in arrays])


def held_in(x, kind=pltpu.VMEM):
    return kind(x.shape, x.dtype)


def out_far(shape, dtype=F32):
    return (ANY, pltpu.HBM(shape, dtype))


def out_near(shape):
    return (None, pltpu.VMEM(shape, F32))


VOLUME = (2, FIELDS, W, PLANE)
FACE = (ROWS, 128)


def exchange(a, b):
    n = lax.axis_size("blk")
    odd = [(i, (i + 1) % n) for i in range(1, n, 2)]
    return (
        lax.ppermute(a, "blk", [(i, i ^ 1) for i in range(n)]),
        lax.ppermute(b, "blk", odd + [(j, i) for i, j in odd]),
    )


def local(field, velocity, thermo, metric, inlet_rows, row_owner, face_link, face_kind):
    devices = lax.axis_size("les") * lax.axis_size("blk")
    ty = jnp.asarray(second_table(), BF16)
    tz = jnp.asarray(third_tables(), BF16)
    zg = jnp.asarray(third_ghost_table(), BF16)
    pick = jnp.asarray(third_pick_table(), BF16)
    c1, c2 = (TIME_STEP * w for w in SECTION_WEIGHTS)
    link = jnp.transpose(face_link, (2, 0, 1))
    means = [velocity, thermo, metric]
    d_scratch = pltpu.VMEM((2, 2, ROWS, 256), F32)
    strips = pltpu.VMEM((W * W, 128), F32)
    volume = pltpu.VMEM(VOLUME, F32)
    counts = [12, FACE_CAP, FACE_CAP]
    dma = pltpu.SemaphoreType.DMA

    inputs = [row_owner, inlet_rows, link, face_kind, field, pick]
    sent, own, a, b, meta = call(
        first_kernel,
        "first_faces",
        [],
        [out_far((devices, 8, 128))]
        + [out_far((n,) + FACE) for n in counts]
        + [out_far((2, 12), jnp.int32)],
        [
            held_in(row_owner, pltpu.SMEM),
            pltpu.SMEM((devices,), jnp.int32),
            held_in(link, pltpu.SMEM),
            held_in(face_kind, pltpu.SMEM),
            pltpu.SMEM((2, 12), jnp.int32),
            held_in(inlet_rows),
            pltpu.VMEM((4, inlet_rows.shape[1], 128), F32),
            pltpu.VMEM((devices, 8, 128), F32),
            volume,
            held_in(pick),
            pltpu.VMEM((12,) + FACE, F32),
            strips,
            dma((9,)),
            dma((2,)),
            dma((12,)),
        ],
        10**9,
        remote=inputs,
    )
    a, b = exchange(a, b)
    got = lax.all_to_all(sent, ("les", "blk"), split_axis=0, concat_axis=0, tiled=True)
    scalars = [meta, link, face_kind]
    inputs = [own, a, b, zg, ty, tz, field] + means
    (pre,) = call(
        functools.partial(section_kernel, c1),
        "section_first",
        [],
        [out_far(VOLUME)],
        [held_in(x, pltpu.SMEM) for x in scalars]
        + [held_in(x) for x in inputs]
        + [volume]
        + GHOST_SCRATCH
        + [d_scratch, dma((13,)), dma((2,))],
        8 * 10**9,
        12 * 10**6,
        remote=scalars + inputs,
    )
    got = got.reshape(devices * 8, 128)
    inputs = [got, pre, field, pick]
    section, middle, own, a, b, src = call(
        functools.partial(middle_kernel, c1),
        "middle_faces",
        [],
        [out_near(VOLUME), out_near(VOLUME)]
        + [out_near((n,) + FACE) for n in counts]
        + [out_near((2, 2, 8, 128 * TILES))],
        [held_in(meta, pltpu.SMEM)]
        + [held_in(x) for x in inputs]
        + [strips, pltpu.VMEM((W * 8, 128), F32), dma((5,))],
        2 * 10**9,
        6 * 10**6,
        remote=[meta] + inputs,
    )
    a, b = exchange(a, b)
    part, first = call(
        functools.partial(interior_kernel, c2),
        "interior",
        [middle, section] + means + [ty, tz],
        [out_near(VOLUME), out_far(VOLUME)],
        [d_scratch, dma],
        6 * 10**9,
        12 * 10**6,
    )
    (second,) = call(
        functools.partial(last_kernel, c2),
        "section_last",
        [own, a, b, part] + means + [zg, src],
        [out_far(VOLUME)],
        GHOST_SCRATCH + [d_scratch, volume, dma((2,))],
        2 * 10**9,
        smem=scalars,
    )
    return first, second


def solution(mesh):
    both = ("les", "blk")
    return jax.shard_map(
        local,
        mesh=mesh,
        in_specs=(
            P(both, None, None, None),
            P(both, None, None, None),
            P(both, None, None, None),
            P(both, None, None, None),
            P(None, both, None),
            P(both),
            P(both, None, None),
            P(both, None),
        ),
        out_specs=(P(both, None, None, None), P(both, None, None, None)),
        check_vma=False,
    )
```

```python
import functools

import jax
import jax.numpy as jnp
import numpy as np
from jax import lax
from jax.experimental import pallas as pl
from jax.experimental.pallas import tpu as pltpu
from jax.sharding import PartitionSpec as P

CAP = 2
FACE_CAP = 4
W = 40
PLANE = W * W
FIELDS = 5
ROWS = FIELDS * W
TILES = 13
INTS = (45.0, -9.0, 1.0)
GAMMA_GAS = 1.4
TIME_STEP = 0.5
SECTION_WEIGHTS = (0.117979901, 0.184646966)
VMEM_LIMIT = 28 * 1024 * 1024
F32 = jnp.float32
BF16 = jnp.bfloat16


def weight_of(offset):
    total = np.zeros(offset.shape, np.float32)
    for step in range(3):
        total += INTS[step] * ((offset == step + 1).astype(np.float32) - (offset == -step - 1))
    return total


def second_table():
    k = np.arange(512)[:, None] - 128
    lane = np.arange(256)[None, :]
    gap = k - lane
    return weight_of(np.where(gap % W == 0, gap // W, 99))


def third_tables():
    tables = []
    for n in range(5):
        k = np.arange(512)[:, None] - 128 + 256 * n
        lane = np.arange(256)[None, :] + 256 * n
        same = (k // W) == (lane // W)
        tables.append(weight_of(np.where(same, k - lane, 99)))
    return np.stack(tables)


def third_ghost_table():
    lane = np.arange(PLANE)[None, :]
    out = np.zeros((256, PLANE), np.float32)
    edge = np.arange(3 * W)[:, None]
    depth, across = edge // W, edge % W
    match = across == lane // W
    out[: 3 * W] = match * weight_of(-1 - depth - lane % W)
    out[128 : 128 + 3 * W] = match * weight_of(W + depth - lane % W)
    return out


def third_pick_table():
    lane = np.arange(PLANE)[:, None]
    out = np.zeros((PLANE, 256), np.float32)
    edge = np.arange(3 * W)[None, :]
    depth, across = edge // W, edge % W
    match = across == lane // W
    out[:, : 3 * W] = match & (lane % W == depth)
    out[:, 128 : 128 + 3 * W] = match & (lane % W == W - 1 - depth)
    return out


def iota(shape, dim):
    return lax.broadcasted_iota(jnp.int32, shape, dim)


def split3(x):
    high = x.astype(BF16)
    rest = x - high.astype(F32)
    mid = rest.astype(BF16)
    low = (rest - mid.astype(F32)).astype(BF16)
    return high, mid, low


def product3(x, table):
    total = None
    for part in split3(x):
        term = jnp.dot(part, table, preferred_element_type=F32)
        total = term if total is None else total + term
    return total


def roll_lanes(x, by):
    by = by % 128
    return x if by == 0 else pltpu.roll(x, by, x.ndim - 1)


def lane_tile(ref, lead, rows, t):
    if t < 12:
        return ref[lead + (rows, pl.ds(128 * t, 128))]
    part = ref[lead + (rows, pl.ds(1536, 64))]
    return jnp.concatenate([part, jnp.zeros(part.shape[:-1] + (64,), F32)], axis=-1)


def combine(dx, dy, dz, velocity, thermo, metric, scale):
    density, pressure = thermo
    carried = [None] * FIELDS
    spread = None
    inverse = 1.0 / density
    extra = {}
    for d, grad in enumerate((dx, dy, dz)):
        if grad is None:
            continue
        m = metric[d] * scale
        a = velocity[d] * m
        for f in range(FIELDS):
            term = a * grad[f]
            carried[f] = term if carried[f] is None else carried[f] + term
        term = m * grad[1 + d]
        spread = term if spread is None else spread + term
        extra[1 + d] = (m * inverse) * grad[4]
    out = [carried[0] + density * spread]
    for f in (1, 2, 3):
        out.append(carried[f] + extra[f] if f in extra else carried[f])
    out.append(carried[4] + (GAMMA_GAS * pressure) * spread)
    return out


def extract(x_ref, block, pick_ref, own_ref, strips):
    base = 6 * block
    lane = iota((W, 128), 1)
    for f in range(FIELDS):
        rows = pl.ds(f * W, W)
        own_ref[base + 2, rows, :] = x_ref[block, f, :, pl.ds(0, 128)]
        b = lane_tile(x_ref, (block, f), pl.ds(0, W), 11)
        a = lane_tile(x_ref, (block, f), pl.ds(0, W), 12)
        middle = jnp.where(lane < 56, roll_lanes(b, 56), roll_lanes(a, 56))
        own_ref[base + 3, rows, :] = jnp.where(
            lane < 40, roll_lanes(a, -24), jnp.where(lane < 80, middle, roll_lanes(b, 8))
        )
    picked = product3(x_ref[block].reshape(ROWS, PLANE), pick_ref[...])
    own_ref[base + 4] = picked[:, :128]
    own_ref[base + 5] = picked[:, 128:]
    sub = iota((8, 128), 0)
    lane8 = iota((8, 128), 1)
    for t in range(TILES):
        for f in range(FIELDS):
            low = lane_tile(x_ref, (block, f), pl.ds(0, 8), t)
            high = lane_tile(x_ref, (block, f), pl.ds(32, 8), t)
            both = jnp.where(sub < 4, low, high)
            for y in range(W):
                start = W * y - 128 * t
                if start >= 0 and start < 128:
                    value = roll_lanes(both, -start)
                    strips[pl.ds(y * W + f * 8, 8), :] = value
                elif start < 0 and start + W > 0:
                    value = roll_lanes(both, -start)
                    old = strips[pl.ds(y * W + f * 8, 8), :]
                    strips[pl.ds(y * W + f * 8, 8), :] = jnp.where(lane8 < -start, old, value)
    for f in range(FIELDS):
        rows = pl.ds(f * W, W)
        for side in range(2):
            parts = []
            for k in range(3):
                row = f * 8 + (7 - k if side else k)
                parts.append(roll_lanes(strips[pl.ds(row, W, stride=W), :], W * k))
            own_ref[base + side, rows, :] = jnp.where(
                lane < 40, parts[0], jnp.where(lane < 80, parts[1], parts[2])
            )


def hand_out(own_ref, a_ref, b_ref, meta_ref):
    for face in range(12):
        place = meta_ref[1, face]

        @pl.when((place >= 1) & (place < 1 + FACE_CAP))
        def _():
            a_ref[place - 1] = own_ref[face]

        @pl.when(place >= 1 + FACE_CAP)
        def _():
            b_ref[place - 1 - FACE_CAP] = own_ref[face]


def flatten_strips(strips, write):
    lane = iota((W, 128), 1)
    for t in range(TILES):
        total = None
        for y in range(W):
            start = W * y - 128 * t
            if start + W <= 0 or start >= 128:
                continue
            value = roll_lanes(strips[pl.ds(y * W, W), :], start)
            if total is None:
                total = value
            else:
                total = jnp.where(lane >= start, value, total)
        write(t, total)


def second_ghosts(face_low, face_high, yg):
    lane = iota((W, 128), 1)

    def near(face):
        first = INTS[0] * face + INTS[1] * roll_lanes(face, -40) + INTS[2] * roll_lanes(face, -80)
        second = INTS[1] * roll_lanes(face, 40) + INTS[2] * face
        third = INTS[2] * roll_lanes(face, 80)
        return jnp.where(
            lane < 40,
            first,
            jnp.where(lane < 80, second, jnp.where(lane < 120, third, jnp.zeros_like(face))),
        )

    for f in range(FIELDS):
        rows = pl.ds(f * W, W)
        yg[0, rows, :] = -near(face_low(rows))
        value = near(face_high(rows))
        crossing = roll_lanes(value, -56)
        zero = jnp.zeros_like(value)
        yg[1, rows, :] = jnp.where(
            lane >= 112, crossing, jnp.where(lane >= 72, roll_lanes(value, -8), zero)
        )
        yg[2, rows, :] = jnp.where(
            lane < 24, crossing, jnp.where(lane < 64, roll_lanes(value, 24), zero)
        )


def turn_face(own_ref, a_ref, b_ref, source, code, keep, faces, slot, swapped):
    @pl.when(source < 12)
    def _():
        swapped[...] = own_ref[source]

    @pl.when((source >= 12) & (source < 12 + FACE_CAP))
    def _():
        swapped[...] = a_ref[source - 12]

    @pl.when(source >= 12 + FACE_CAP)
    def _():
        swapped[...] = b_ref[source - 12 - FACE_CAP]

    @pl.when(code >= 4)
    def _():
        lane = iota((W, 128), 1)
        whole = jnp.concatenate([swapped[...], jnp.zeros((56, 128), F32)], axis=0)
        left = jnp.transpose(whole[:128])
        right = jnp.transpose(whole[128:])
        for f in range(FIELDS):
            parts = []
            for k in range(3):
                rows = slice(k * W, k * W + W)
                shift = W * k - W * f
                if f < 3:
                    piece = left[rows]
                elif f == 3:
                    piece = jnp.where(lane >= 120, left[rows], right[rows])
                else:
                    piece = right[rows]
                parts.append(roll_lanes(piece, shift))
            swapped[pl.ds(f * W, W), :] = jnp.where(
                lane < 40, parts[0], jnp.where(lane < 80, parts[1], parts[2])
            )

    flip_a = code % 2
    flip_b = (code // 2) % 2
    lane = iota((8, 128), 1)
    depth = (lane >= 40).astype(jnp.int32) + (lane >= 80).astype(jnp.int32)
    mirrored = jnp.where(lane < 120, 2 * W * depth + (W - 1) - lane, lane)
    lane_index = jnp.where(flip_b == 1, mirrored, lane)
    sub = iota((8, 128), 0)
    sub_index = jnp.where(flip_a == 1, 7 - sub, sub)
    for f in range(FIELDS):
        for g in range(5):
            start = f * W + 8 * jnp.where(flip_a == 1, 4 - g, g)
            value = swapped[pl.ds(pl.multiple_of(start, 8), 8), :]
            value = jnp.take_along_axis(value, lane_index, axis=1, mode="promise_in_bounds")
            value = jnp.take_along_axis(value, sub_index, axis=0, mode="promise_in_bounds")
            faces[slot, pl.ds(f * W + 8 * g, 8), :] = value * keep


def prepare_ghosts(block, meta_ref, link_ref, kind_ref, own_ref, a_ref, b_ref, scratch):
    faces, swapped, strips, yg, flat = scratch
    for face in range(6):
        keep = jnp.where(kind_ref[block, face] == 2, 0.0, 1.0).astype(F32)
        turn_face(
            own_ref,
            a_ref,
            b_ref,
            meta_ref[0, block * 6 + face],
            link_ref[2, block, face],
            keep,
            faces,
            face,
            swapped.at[face],
        )
    second_ghosts(lambda rows: faces[2, rows, :], lambda rows: faces[3, rows, :], yg)
    for f in range(FIELDS):
        for side in range(2):
            value = faces[side, pl.ds(f * W, W), :]
            for k in range(3):
                row = f * 8 + (7 - k if side else k)
                strips[pl.ds(row, W, stride=W), :] = roll_lanes(value, -W * k)

    def write(t, value):
        flat[:, pl.ds(128 * t, 128)] = value

    flatten_strips(strips, write)


GHOST_SCRATCH = [
    pltpu.VMEM((6, ROWS, 128), F32),
    pltpu.VMEM((6, ROWS, 128), F32),
    pltpu.VMEM((W * W, 128), F32),
    pltpu.VMEM((3, ROWS, 128), F32),
    pltpu.VMEM((W, 128 * TILES), F32),
]


def add(a, b):
    return b if a is None else a + b


def inner_first(x_ref, block, f, g, lanes, w):
    sub = iota((8, w), 0)
    cur = x_ref[block, f, pl.ds(8 * g, 8), lanes]
    zero = jnp.zeros_like(cur)
    before = x_ref[block, f, pl.ds(8 * g - 8, 8), lanes] if g > 0 else zero
    after = x_ref[block, f, pl.ds(8 * g + 8, 8), lanes] if g < 4 else zero
    total = None
    for j in (1, 2, 3):
        plus = pltpu.roll(jnp.where(sub >= j, cur, after), 8 - j, 0)
        minus = pltpu.roll(jnp.where(sub < 8 - j, cur, before), j, 0)
        total = add(total, INTS[j - 1] * (plus - minus))
    return total


def ghost_first(flat, f, g, lanes, w):
    sub = iota((8, w), 0)
    ghost = [flat[pl.ds(f * 8 + (7 - k if g else k), 1), lanes] for k in range(3)]
    far = (7 - sub) if g else sub
    total = jnp.zeros((8, w), F32)
    for m in range(3):
        row = None
        for k in range(3 - m):
            row = add(row, INTS[m + k] * ghost[k])
        total = jnp.where(far == m, row, total)
    return total if g else -total


def sweep(block, scale, x_ref, tables, ghosts, means, d_ref, emit):
    vel_ref, th_ref, me_ref = means
    if ghosts is not None:
        faces, _, _, yg, flat, zg_ref = ghosts
        edge = split3(jnp.concatenate([faces[4], faces[5]], axis=1))
    for n in range(7):
        wide = min(256, PLANE - 256 * n)
        slot = n % 2
        along = [None, None]
        if x_ref is not None:
            ty_ref, tz_ref = tables
            low = max(0, 256 * n - 128)
            high = min(PLANE, 256 * n + 384)
            skip = low - (256 * n - 128)
            size = high - low
            parts = split3(x_ref[block, :, :, pl.ds(low, size)].reshape(ROWS, size))
            ty = ty_ref[pl.ds(skip, size), pl.ds(0, wide)]
            tz = tz_ref[n % 5, pl.ds(skip, size), pl.ds(0, wide)]
            for part in parts:
                along[0] = add(along[0], jnp.dot(part, ty, preferred_element_type=F32))
                along[1] = add(along[1], jnp.dot(part, tz, preferred_element_type=F32))
        if ghosts is not None:
            table = zg_ref[:, pl.ds(256 * n, wide)]
            for part in edge:
                along[1] = add(along[1], jnp.dot(part, table, preferred_element_type=F32))
        for which in range(2):
            if along[which] is not None:
                d_ref[slot, which, :, pl.ds(0, wide)] = along[which]
        for at in range(0, wide, 128):
            w = min(128, wide - at)
            t = 2 * n + at // 128
            lanes = pl.ds(128 * t, w)
            for g in range(5):
                rows = pl.ds(8 * g, 8)
                dx, dy, dz = [], [], []
                for f in range(FIELDS):
                    own_rows = pl.ds(f * W + 8 * g, 8)
                    x = y = None
                    if x_ref is not None:
                        x = inner_first(x_ref, block, f, g, lanes, w)
                        y = d_ref[slot, 0, own_rows, pl.ds(at, w)]
                    if ghosts is not None:
                        if g in (0, 4):
                            x = add(x, ghost_first(flat, f, g, lanes, w))
                        if t in (0, 11, 12):
                            y = add(y, yg[{0: 0, 11: 1, 12: 2}[t], own_rows, pl.ds(0, w)])
                    dx.append(x)
                    dy.append(y)
                    dz.append(d_ref[slot, 1, own_rows, pl.ds(at, w)])
                out = combine(
                    dx if dx[0] is not None else None,
                    dy if dy[0] is not None else None,
                    dz,
                    [vel_ref[block, d, rows, lanes] for d in range(3)],
                    [th_ref[block, d, rows, lanes] for d in range(2)],
                    [me_ref[block, d, rows, lanes] for d in range(3)],
                    scale / 60.0,
                )
                for f in range(FIELDS):
                    emit(f, g, rows, lanes, w, out[f])


def both_blocks(body):
    def step(block, carry):
        body(block)
        return carry

    lax.fori_loop(0, 2, step, 0)


def pack(owner_ref, rows_ref, out_ref, count, wide):
    devices = out_ref.shape[0]
    rows = owner_ref.shape[0]
    sub = iota((8, 128), 0)
    lane = iota((8, 128), 1)
    empty = jnp.where((sub % 4 == 1) & (lane == 127), -1.0, 0.0).astype(F32)
    wide[...] = jnp.zeros_like(wide)
    for s in range(2):
        wide[2 * s] = rows_ref[s, :, pl.ds(0, 128)]
        wide[2 * s + 1, :, pl.ds(0, 72)] = rows_ref[s, :, pl.ds(128, 72)]

    def clear(d, carry):
        count[d] = 0
        out_ref[d] = empty
        return carry

    lax.fori_loop(0, devices, clear, 0, unroll=8)
    lane1 = iota((1, 128), 1)

    def place(i, carry):
        line = owner_ref[i]
        target = lax.shift_right_logical(line * 52429, 22)
        local = (line - target * (2 * W)).astype(F32)
        slot = count[target]
        count[target] = slot + 1
        for s in range(2):
            for j in range(2):
                value = wide[2 * s + j, pl.ds(i, 1), :]
                if s == 0 and j == 1:
                    value = jnp.where(lane1 == 127, local, value)
                out_ref[target, pl.ds(4 * slot + 2 * s + j, 1), :] = value
        return carry

    lax.fori_loop(0, rows, place, 0, unroll=8)


def first_kernel(
    owner_hbm,
    rows_hbm,
    link_hbm,
    kind_hbm,
    x_hbm,
    pick_hbm,
    sent_hbm,
    own_hbm,
    a_hbm,
    b_hbm,
    meta_hbm,
    owner_ref,
    count,
    link_ref,
    kind_ref,
    meta_ref,
    rows_ref,
    wide,
    sent,
    x_ref,
    pick_ref,
    own_ref,
    strips,
    sems,
    own_sems,
    hand_sems,
):
    loads = [
        pltpu.make_async_copy(*pair, sems.at[i])
        for i, pair in enumerate(
            [
                (owner_hbm, owner_ref),
                (rows_hbm, rows_ref),
                (link_hbm, link_ref),
                (kind_hbm, kind_ref),
                (pick_hbm, pick_ref),
                (x_hbm.at[0], x_ref.at[0]),
                (x_hbm.at[1], x_ref.at[1]),
            ]
        )
    ]
    for load in loads:
        load.start()
    for load in loads[:4]:
        load.wait()
    pack(owner_ref, rows_ref, sent, count, wide)
    send = pltpu.make_async_copy(sent, sent_hbm, sems.at[7])
    send.start()
    cycle = lax.axis_size("blk")
    row_start = lax.axis_index("les") * cycle
    column = lax.axis_index("blk")
    above = row_start + lax.rem(column + 1, cycle)
    below = row_start + lax.rem(column + cycle - 1, cycle)
    even = lax.rem(column, 2) == 0
    partner_a = jnp.where(even, above, below)
    partner_b = jnp.where(even, below, above)
    partner, to_a, to_b = [], [], []
    count_a = jnp.int32(0)
    count_b = jnp.int32(0)
    for i in range(12):
        target = link_ref[0, i // 6, i % 6]
        device = lax.shift_right_logical(target, 1)
        linked = kind_ref[i // 6, i % 6] == 0
        is_a = linked & (device == partner_a)
        is_b = linked & (device == partner_b)
        partner.append((target - 2 * device) * 6 + link_ref[1, i // 6, i % 6])
        to_a.append(is_a)
        to_b.append(is_b)
        meta_ref[1, i] = jnp.where(is_a, 1 + count_a, jnp.where(is_b, 1 + FACE_CAP + count_b, 0))
        count_a = count_a + is_a.astype(jnp.int32)
        count_b = count_b + is_b.astype(jnp.int32)
    for i in range(12):
        rank_a = jnp.int32(0)
        rank_b = jnp.int32(0)
        for j in range(12):
            less = partner[j] < partner[i]
            rank_a = rank_a + (to_a[j] & less).astype(jnp.int32)
            rank_b = rank_b + (to_b[j] & less).astype(jnp.int32)
        meta_ref[0, i] = jnp.where(
            to_a[i], 12 + rank_a, jnp.where(to_b[i], 12 + FACE_CAP + rank_b, partner[i])
        )
    meta_out = pltpu.make_async_copy(meta_ref, meta_hbm, sems.at[8])
    meta_out.start()
    for load in loads[4:]:
        load.wait()

    def copies(face):
        place = meta_ref[1, face]
        return (
            (place >= 1) & (place < 1 + FACE_CAP),
            lambda: pltpu.make_async_copy(
                own_ref.at[face], a_hbm.at[place - 1], hand_sems.at[face]
            ),
            place >= 1 + FACE_CAP,
            lambda: pltpu.make_async_copy(
                own_ref.at[face], b_hbm.at[place - 1 - FACE_CAP], hand_sems.at[face]
            ),
        )

    def keep(block):
        return pltpu.make_async_copy(
            own_ref.at[pl.ds(6 * block, 6)], own_hbm.at[pl.ds(6 * block, 6)], own_sems.at[block]
        )

    def body(block):
        extract(x_ref, block, pick_ref, own_ref, strips)
        for i in range(6):
            is_a, copy_a, is_b, copy_b = copies(6 * block + i)

            @pl.when(is_a)
            def _():
                copy_a().start()

            @pl.when(is_b)
            def _():
                copy_b().start()

        keep(block).start()

    both_blocks(body)
    for face in range(12):
        is_a, copy_a, is_b, copy_b = copies(face)

        @pl.when(is_a)
        def _():
            copy_a().wait()

        @pl.when(is_b)
        def _():
            copy_b().wait()

    for block in range(2):
        keep(block).wait()
    send.wait()
    meta_out.wait()


def load_all(pairs, sems):
    loads = [pltpu.make_async_copy(*pair, sems.at[i]) for i, pair in enumerate(pairs)]
    for load in loads:
        load.start()
    return loads


def inner_kernel(scale, *refs):
    sources = refs[:6]
    part, vel, th, me = refs[6:10]
    ty, tz, x_ref, d_ref, sems = refs[10:15]
    pairs = [[(sources[0], ty), (sources[1], tz)], []]
    for block in range(2):
        for source, target in zip(sources[2:], (x_ref, vel, th, me)):
            pairs[block].append((source.at[block], target.at[block]))
    loads = load_all(pairs[0] + pairs[1], sems)

    def body(block):
        @pl.when(block == 0)
        def _():
            for load in loads[:6]:
                load.wait()

        @pl.when(block == 1)
        def _():
            for load in loads[6:]:
                load.wait()

        def emit(f, g, rows, lanes, w, value):
            part[block, f, rows, lanes] = -value

        sweep(block, scale, x_ref, (ty, tz), None, (vel, th, me), d_ref, emit)

    both_blocks(body)


def inject(got_ref, src, strips):
    rows = got_ref.shape[0] // 4
    lane = iota((rows, 128), 1)
    parts = [got_ref[pl.ds(j, rows, stride=4), :] for j in range(4)]
    label = jnp.max(jnp.where(lane == 127, parts[1], -1.0), axis=1, keepdims=True)
    chosen = jnp.where(label == lane.astype(F32), 1.0, 0.0)
    chooser = jnp.transpose(chosen).astype(BF16)
    lane = iota((W, 128), 1)
    lane8 = iota((8, 128), 1)
    for s in range(2):
        sums = []
        for j in range(2):
            total = None
            for part in split3(parts[2 * s + j]):
                total = add(total, jnp.dot(chooser, part, preferred_element_type=F32))
            sums.append(total)
        for b in range(2):
            left, right = (value[b * W : b * W + W] for value in sums)
            for f in range(FIELDS):
                if f < 3:
                    piece = left
                elif f == 3:
                    piece = jnp.where(lane >= 120, left, right)
                else:
                    piece = right
                strips[pl.ds(f, W, stride=8), :] = roll_lanes(piece, -W * f)
            for t in range(TILES):
                total = None
                for y in range(W):
                    start = W * y - 128 * t
                    if start + W <= 0 or start >= 128:
                        continue
                    value = roll_lanes(strips[pl.ds(y * 8, 8), :], start)
                    total = value if total is None else jnp.where(lane8 >= start, value, total)
                src[s, b, :, pl.ds(128 * t, 128)] = total


def middle_kernel(scale, *refs):
    sources, got, outs = refs[:4], refs[4], refs[5:11]
    section, mid, own, a, b, src = outs
    held, strips, lines, sems = refs[11:15], refs[15], refs[16], refs[17]
    loads = load_all(zip(sources, held), sems)
    meta, pre, q_ref, pick = held
    inject(got, src, lines)
    for load in loads:
        load.wait()

    def body(block):
        for f in range(FIELDS):
            value = pre[block, f]
            line = scale * src[0, block, pl.ds(f, 1), pl.ds(0, PLANE)]
            top = value[:8]
            top = jnp.where(iota((8, PLANE), 0) == 0, top + line, top)
            section[block, f, pl.ds(0, 8), :] = top
            section[block, f, pl.ds(8, W - 8), :] = value[8:]
            mid[block, f, pl.ds(0, 8), :] = q_ref[block, f, pl.ds(0, 8), :] + top
            mid[block, f, pl.ds(8, W - 8), :] = q_ref[block, f, pl.ds(8, W - 8), :] + value[8:]
        extract(mid, block, pick, own, strips)

    both_blocks(body)
    hand_out(own, a, b, meta)


def interior_kernel(scale, x_ref, section, vel, th, me, ty, tz, part, out_hbm, d_ref, sem):
    copy = pltpu.make_async_copy(section, out_hbm, sem)
    copy.start()

    def body(block):
        def emit(f, g, rows, lanes, w, value):
            part[block, f, rows, lanes] = -value

        sweep(block, scale, x_ref, (ty, tz), None, (vel, th, me), d_ref, emit)

    both_blocks(body)
    copy.wait()


def ghost_kernel(scale, last, *refs):
    meta, link, kind, own, a, b, part, vel, th, me, zg = refs[:11]
    src = refs[11] if last else None
    refs = refs[11 + last :]
    out_hbm, ghost, d_ref, out, sems = refs[0], refs[1:6], refs[6], refs[7], refs[8]

    def copy(block):
        return pltpu.make_async_copy(out.at[block], out_hbm.at[block], sems.at[block])

    def body(block):
        prepare_ghosts(block, meta, link, kind, own, a, b, ghost)

        def emit(f, g, rows, lanes, w, value):
            value = part[block, f, rows, lanes] - value
            if last and g == 0:
                line = scale * src[1, block, pl.ds(f, 1), lanes]
                value = jnp.where(iota((8, w), 0) == 0, value + line, value)
            out[block, f, rows, lanes] = value

        sweep(block, scale, None, None, tuple(ghost) + (zg,), (vel, th, me), d_ref, emit)
        copy(block).start()

    both_blocks(body)
    for block in range(2):
        copy(block).wait()


SMEM = pl.BlockSpec(memory_space=pltpu.SMEM)
VMEM = pl.BlockSpec(memory_space=pltpu.VMEM)
ANY = pl.BlockSpec(memory_space=pl.ANY)


def near(x):
    return pltpu.with_memory_space_constraint(x, pltpu.VMEM)


def far(x):
    return pltpu.with_memory_space_constraint(x, pltpu.HBM)


def cost(flops, size):
    return pl.CostEstimate(flops=flops, bytes_accessed=size, transcendentals=0)


def call(kernel, name, arrays, outs, scratch, flops=0, size=10**6, smem=(), remote=()):
    specs = [VMEM if spot is None else spot for spot, _ in outs]
    return pl.pallas_call(
        kernel,
        in_specs=[SMEM] * len(smem) + [ANY] * len(remote) + [VMEM] * len(arrays),
        out_specs=specs,
        out_shape=[shape for _, shape in outs],
        scratch_shapes=scratch,
        compiler_params=pltpu.CompilerParams(vmem_limit_bytes=VMEM_LIMIT),
        cost_estimate=cost(flops, size),
        name=name,
    )(*smem, *[far(x) for x in remote], *[near(x) for x in arrays])


def held_in(x, kind=pltpu.VMEM):
    return kind(x.shape, x.dtype)


def out_far(shape, dtype=F32):
    return (ANY, pltpu.HBM(shape, dtype))


def out_near(shape):
    return (None, pltpu.VMEM(shape, F32))


VOLUME = (2, FIELDS, W, PLANE)
FACE = (ROWS, 128)


def exchange(a, b):
    n = lax.axis_size("blk")
    odd = [(i, (i + 1) % n) for i in range(1, n, 2)]
    return (
        lax.ppermute(a, "blk", [(i, i ^ 1) for i in range(n)]),
        lax.ppermute(b, "blk", odd + [(j, i) for i, j in odd]),
    )


def local(field, velocity, thermo, metric, inlet_rows, row_owner, face_link, face_kind):
    devices = lax.axis_size("les") * lax.axis_size("blk")
    ty = jnp.asarray(second_table(), BF16)
    tz = jnp.asarray(third_tables(), BF16)
    zg = jnp.asarray(third_ghost_table(), BF16)
    pick = jnp.asarray(third_pick_table(), BF16)
    c1, c2 = (TIME_STEP * w for w in SECTION_WEIGHTS)
    link = jnp.transpose(face_link, (2, 0, 1))
    means = [velocity, thermo, metric]
    d_scratch = pltpu.VMEM((2, 2, ROWS, 256), F32)
    strips = pltpu.VMEM((W * W, 128), F32)
    volume = pltpu.VMEM(VOLUME, F32)
    counts = [12, FACE_CAP, FACE_CAP]
    dma = pltpu.SemaphoreType.DMA

    inputs = [row_owner, inlet_rows, link, face_kind, field, pick]
    sent, own, a, b, meta = call(
        first_kernel,
        "first_faces",
        [],
        [out_far((devices, 8, 128))]
        + [out_far((n,) + FACE) for n in counts]
        + [out_far((2, 12), jnp.int32)],
        [
            held_in(row_owner, pltpu.SMEM),
            pltpu.SMEM((devices,), jnp.int32),
            held_in(link, pltpu.SMEM),
            held_in(face_kind, pltpu.SMEM),
            pltpu.SMEM((2, 12), jnp.int32),
            held_in(inlet_rows),
            pltpu.VMEM((4, inlet_rows.shape[1], 128), F32),
            pltpu.VMEM((devices, 8, 128), F32),
            volume,
            held_in(pick),
            pltpu.VMEM((12,) + FACE, F32),
            strips,
            dma((9,)),
            dma((2,)),
            dma((12,)),
        ],
        10**9,
        remote=inputs,
    )
    a, b = exchange(a, b)
    got = lax.all_to_all(sent, ("les", "blk"), split_axis=0, concat_axis=0, tiled=True)
    scalars = [meta, link, face_kind]
    ghost_scratch = GHOST_SCRATCH + [d_scratch, volume, dma((2,))]
    part, *means = call(
        functools.partial(inner_kernel, c1),
        "inner_first",
        [],
        [out_near(x.shape) for x in [field] + means],
        [held_in(ty), held_in(tz), volume, d_scratch, dma((10,))],
        100000000,
        1000000,
        remote=[ty, tz, field] + means,
    )
    (pre,) = call(
        functools.partial(ghost_kernel, c1, False),
        "ghosts_first",
        [own, a, b, part] + means + [zg],
        [out_far(VOLUME)],
        ghost_scratch,
        2000000000,
        1000000,
        smem=scalars,
    )
    got = got.reshape(devices * 8, 128)
    inputs = [meta, pre, field, pick]
    section, middle, own, a, b, src = call(
        functools.partial(middle_kernel, c1),
        "middle_faces",
        [got],
        [out_near(VOLUME), out_near(VOLUME)]
        + [out_near((n,) + FACE) for n in counts]
        + [out_near((2, 2, 8, 128 * TILES))],
        [held_in(meta, pltpu.SMEM)]
        + [held_in(x) for x in inputs[1:]]
        + [strips, pltpu.VMEM((W * 8, 128), F32), dma((4,))],
        2 * 10**9,
        6 * 10**6,
        remote=inputs,
    )
    means = [velocity, thermo, metric]
    a, b = exchange(a, b)
    part, first = call(
        functools.partial(interior_kernel, c2),
        "interior",
        [middle, section] + means + [ty, tz],
        [out_near(VOLUME), out_far(VOLUME)],
        [d_scratch, dma],
        6 * 10**9,
        12 * 10**6,
    )
    (second,) = call(
        functools.partial(ghost_kernel, c2, True),
        "ghosts_last",
        [own, a, b, part] + means + [zg, src],
        [out_far(VOLUME)],
        ghost_scratch,
        2 * 10**9,
        smem=scalars,
    )
    return first, second


def solution(mesh):
    both = ("les", "blk")
    return jax.shard_map(
        local,
        mesh=mesh,
        in_specs=(
            P(both, None, None, None),
            P(both, None, None, None),
            P(both, None, None, None),
            P(both, None, None, None),
            P(None, both, None),
            P(both),
            P(both, None, None),
            P(both, None),
        ),
        out_specs=(P(both, None, None, None), P(both, None, None, None)),
        check_vma=False,
    )
```

```python
import functools

import jax
import jax.numpy as jnp
import numpy as np
from jax import lax
from jax.experimental import pallas as pl
from jax.experimental.pallas import tpu as pltpu
from jax.sharding import PartitionSpec as P

CAP = 2
FACE_CAP = 4
W = 40
PLANE = W * W
FIELDS = 5
ROWS = FIELDS * W
TILES = 13
INTS = (45.0, -9.0, 1.0)
GAMMA_GAS = 1.4
TIME_STEP = 0.5
SECTION_WEIGHTS = (0.117979901, 0.184646966)
VMEM_LIMIT = 28 * 1024 * 1024
F32 = jnp.float32
BF16 = jnp.bfloat16


def weight_of(offset):
    total = np.zeros(offset.shape, np.float32)
    for step in range(3):
        total += INTS[step] * ((offset == step + 1).astype(np.float32) - (offset == -step - 1))
    return total


def second_table():
    k = np.arange(512)[:, None] - 128
    lane = np.arange(256)[None, :]
    gap = k - lane
    return weight_of(np.where(gap % W == 0, gap // W, 99))


def third_tables():
    tables = []
    for n in range(5):
        k = np.arange(512)[:, None] - 128 + 256 * n
        lane = np.arange(256)[None, :] + 256 * n
        same = (k // W) == (lane // W)
        tables.append(weight_of(np.where(same, k - lane, 99)))
    return np.stack(tables)


def third_ghost_table():
    lane = np.arange(PLANE)[None, :]
    out = np.zeros((256, PLANE), np.float32)
    edge = np.arange(3 * W)[:, None]
    depth, across = edge // W, edge % W
    match = across == lane // W
    out[: 3 * W] = match * weight_of(-1 - depth - lane % W)
    out[128 : 128 + 3 * W] = match * weight_of(W + depth - lane % W)
    return out


def third_pick_table():
    lane = np.arange(PLANE)[:, None]
    out = np.zeros((PLANE, 256), np.float32)
    edge = np.arange(3 * W)[None, :]
    depth, across = edge // W, edge % W
    match = across == lane // W
    out[:, : 3 * W] = match & (lane % W == depth)
    out[:, 128 : 128 + 3 * W] = match & (lane % W == W - 1 - depth)
    return out


def iota(shape, dim):
    return lax.broadcasted_iota(jnp.int32, shape, dim)


def split3(x):
    high = x.astype(BF16)
    rest = x - high.astype(F32)
    mid = rest.astype(BF16)
    low = (rest - mid.astype(F32)).astype(BF16)
    return high, mid, low


def product3(x, table):
    total = None
    for part in split3(x):
        term = jnp.dot(part, table, preferred_element_type=F32)
        total = term if total is None else total + term
    return total


def roll_lanes(x, by):
    by = by % 128
    return x if by == 0 else pltpu.roll(x, by, x.ndim - 1)


def lane_tile(ref, lead, rows, t):
    if t < 12:
        return ref[lead + (rows, pl.ds(128 * t, 128))]
    part = ref[lead + (rows, pl.ds(1536, 64))]
    return jnp.concatenate([part, jnp.zeros(part.shape[:-1] + (64,), F32)], axis=-1)


def combine(dx, dy, dz, velocity, thermo, metric, scale):
    density, pressure = thermo
    carried = [None] * FIELDS
    spread = None
    inverse = 1.0 / density
    extra = {}
    for d, grad in enumerate((dx, dy, dz)):
        if grad is None:
            continue
        m = metric[d] * scale
        a = velocity[d] * m
        for f in range(FIELDS):
            term = a * grad[f]
            carried[f] = term if carried[f] is None else carried[f] + term
        term = m * grad[1 + d]
        spread = term if spread is None else spread + term
        extra[1 + d] = (m * inverse) * grad[4]
    out = [carried[0] + density * spread]
    for f in (1, 2, 3):
        out.append(carried[f] + extra[f] if f in extra else carried[f])
    out.append(carried[4] + (GAMMA_GAS * pressure) * spread)
    return out


def extract(x_ref, block, pick_ref, own_ref, strips):
    base = 6 * block
    lane = iota((W, 128), 1)
    for f in range(FIELDS):
        rows = pl.ds(f * W, W)
        own_ref[base + 2, rows, :] = x_ref[block, f, :, pl.ds(0, 128)]
        b = lane_tile(x_ref, (block, f), pl.ds(0, W), 11)
        a = lane_tile(x_ref, (block, f), pl.ds(0, W), 12)
        middle = jnp.where(lane < 56, roll_lanes(b, 56), roll_lanes(a, 56))
        own_ref[base + 3, rows, :] = jnp.where(
            lane < 40, roll_lanes(a, -24), jnp.where(lane < 80, middle, roll_lanes(b, 8))
        )
    picked = product3(x_ref[block].reshape(ROWS, PLANE), pick_ref[...])
    own_ref[base + 4] = picked[:, :128]
    own_ref[base + 5] = picked[:, 128:]
    sub = iota((8, 128), 0)
    lane8 = iota((8, 128), 1)
    for t in range(TILES):
        for f in range(FIELDS):
            low = lane_tile(x_ref, (block, f), pl.ds(0, 8), t)
            high = lane_tile(x_ref, (block, f), pl.ds(32, 8), t)
            both = jnp.where(sub < 4, low, high)
            for y in range(W):
                start = W * y - 128 * t
                if start >= 0 and start < 128:
                    value = roll_lanes(both, -start)
                    strips[pl.ds(y * W + f * 8, 8), :] = value
                elif start < 0 and start + W > 0:
                    value = roll_lanes(both, -start)
                    old = strips[pl.ds(y * W + f * 8, 8), :]
                    strips[pl.ds(y * W + f * 8, 8), :] = jnp.where(lane8 < -start, old, value)
    for f in range(FIELDS):
        rows = pl.ds(f * W, W)
        for side in range(2):
            parts = []
            for k in range(3):
                row = f * 8 + (7 - k if side else k)
                parts.append(roll_lanes(strips[pl.ds(row, W, stride=W), :], W * k))
            own_ref[base + side, rows, :] = jnp.where(
                lane < 40, parts[0], jnp.where(lane < 80, parts[1], parts[2])
            )


def hand_out(own_ref, a_ref, b_ref, meta_ref):
    for face in range(12):
        place = meta_ref[1, face]

        @pl.when((place >= 1) & (place < 1 + FACE_CAP))
        def _():
            a_ref[place - 1] = own_ref[face]

        @pl.when(place >= 1 + FACE_CAP)
        def _():
            b_ref[place - 1 - FACE_CAP] = own_ref[face]


def flatten_strips(strips, write):
    lane = iota((W, 128), 1)
    for t in range(TILES):
        total = None
        for y in range(W):
            start = W * y - 128 * t
            if start + W <= 0 or start >= 128:
                continue
            value = roll_lanes(strips[pl.ds(y * W, W), :], start)
            if total is None:
                total = value
            else:
                total = jnp.where(lane >= start, value, total)
        write(t, total)


def second_ghosts(face_low, face_high, yg):
    lane = iota((W, 128), 1)

    def near(face):
        first = INTS[0] * face + INTS[1] * roll_lanes(face, -40) + INTS[2] * roll_lanes(face, -80)
        second = INTS[1] * roll_lanes(face, 40) + INTS[2] * face
        third = INTS[2] * roll_lanes(face, 80)
        return jnp.where(
            lane < 40,
            first,
            jnp.where(lane < 80, second, jnp.where(lane < 120, third, jnp.zeros_like(face))),
        )

    for f in range(FIELDS):
        rows = pl.ds(f * W, W)
        yg[0, rows, :] = -near(face_low(rows))
        value = near(face_high(rows))
        crossing = roll_lanes(value, -56)
        zero = jnp.zeros_like(value)
        yg[1, rows, :] = jnp.where(
            lane >= 112, crossing, jnp.where(lane >= 72, roll_lanes(value, -8), zero)
        )
        yg[2, rows, :] = jnp.where(
            lane < 24, crossing, jnp.where(lane < 64, roll_lanes(value, 24), zero)
        )


def turn_face(own_ref, a_ref, b_ref, source, code, keep, faces, slot, swapped):
    if own_ref is None:
        swapped[...] = b_ref[source - 12 - FACE_CAP]
    else:

        @pl.when(source < 12)
        def _():
            swapped[...] = own_ref[source]

        @pl.when((source >= 12) & (source < 12 + FACE_CAP))
        def _():
            swapped[...] = a_ref[source - 12]

        if b_ref is not None:

            @pl.when(source >= 12 + FACE_CAP)
            def _():
                swapped[...] = b_ref[source - 12 - FACE_CAP]

    @pl.when(code >= 4)
    def _():
        lane = iota((W, 128), 1)
        whole = jnp.concatenate([swapped[...], jnp.zeros((56, 128), F32)], axis=0)
        left = jnp.transpose(whole[:128])
        right = jnp.transpose(whole[128:])
        for f in range(FIELDS):
            parts = []
            for k in range(3):
                rows = slice(k * W, k * W + W)
                shift = W * k - W * f
                if f < 3:
                    piece = left[rows]
                elif f == 3:
                    piece = jnp.where(lane >= 120, left[rows], right[rows])
                else:
                    piece = right[rows]
                parts.append(roll_lanes(piece, shift))
            swapped[pl.ds(f * W, W), :] = jnp.where(
                lane < 40, parts[0], jnp.where(lane < 80, parts[1], parts[2])
            )

    flip_a = code % 2
    flip_b = (code // 2) % 2
    lane = iota((8, 128), 1)
    depth = (lane >= 40).astype(jnp.int32) + (lane >= 80).astype(jnp.int32)
    mirrored = jnp.where(lane < 120, 2 * W * depth + (W - 1) - lane, lane)
    lane_index = jnp.where(flip_b == 1, mirrored, lane)
    sub = iota((8, 128), 0)
    sub_index = jnp.where(flip_a == 1, 7 - sub, sub)
    for f in range(FIELDS):
        for g in range(5):
            start = f * W + 8 * jnp.where(flip_a == 1, 4 - g, g)
            value = swapped[pl.ds(pl.multiple_of(start, 8), 8), :]
            value = jnp.take_along_axis(value, lane_index, axis=1, mode="promise_in_bounds")
            value = jnp.take_along_axis(value, sub_index, axis=0, mode="promise_in_bounds")
            faces[slot, pl.ds(f * W + 8 * g, 8), :] = value * keep


def prepare_ghosts(
    block, meta_ref, link_ref, kind_ref, own_ref, a_ref, b_ref, scratch, early=None
):
    faces, swapped, strips, yg, flat = scratch
    for face in range(6):
        index = block * 6 + face
        source = meta_ref[0, index]

        def turn():
            keep = jnp.where(kind_ref[block, face] == 2, 0.0, 1.0).astype(F32)
            code = link_ref[2, block, face]
            turn_face(own_ref, a_ref, b_ref, source, code, keep, faces, face, swapped.at[face])

        if early is None:
            turn()
        else:
            pl.when(source >= 12 + FACE_CAP)(turn)

            @pl.when(source < 12 + FACE_CAP)
            def _():
                faces[face] = early[index]

    second_ghosts(lambda rows: faces[2, rows, :], lambda rows: faces[3, rows, :], yg)
    for f in range(FIELDS):
        for side in range(2):
            value = faces[side, pl.ds(f * W, W), :]
            for k in range(3):
                row = f * 8 + (7 - k if side else k)
                strips[pl.ds(row, W, stride=W), :] = roll_lanes(value, -W * k)

    def write(t, value):
        flat[:, pl.ds(128 * t, 128)] = value

    flatten_strips(strips, write)


GHOST_SCRATCH = [
    pltpu.VMEM((6, ROWS, 128), F32),
    pltpu.VMEM((6, ROWS, 128), F32),
    pltpu.VMEM((W * W, 128), F32),
    pltpu.VMEM((3, ROWS, 128), F32),
    pltpu.VMEM((W, 128 * TILES), F32),
]


def add(a, b):
    return b if a is None else a + b


def inner_first(x_ref, block, f, g, lanes, w):
    sub = iota((8, w), 0)
    cur = x_ref[block, f, pl.ds(8 * g, 8), lanes]
    zero = jnp.zeros_like(cur)
    before = x_ref[block, f, pl.ds(8 * g - 8, 8), lanes] if g > 0 else zero
    after = x_ref[block, f, pl.ds(8 * g + 8, 8), lanes] if g < 4 else zero
    total = None
    for j in (1, 2, 3):
        plus = pltpu.roll(jnp.where(sub >= j, cur, after), 8 - j, 0)
        minus = pltpu.roll(jnp.where(sub < 8 - j, cur, before), j, 0)
        total = add(total, INTS[j - 1] * (plus - minus))
    return total


def ghost_first(flat, f, g, lanes, w):
    sub = iota((8, w), 0)
    ghost = [flat[pl.ds(f * 8 + (7 - k if g else k), 1), lanes] for k in range(3)]
    far = (7 - sub) if g else sub
    total = jnp.zeros((8, w), F32)
    for m in range(3):
        row = None
        for k in range(3 - m):
            row = add(row, INTS[m + k] * ghost[k])
        total = jnp.where(far == m, row, total)
    return total if g else -total


def sweep(block, scale, x_ref, tables, ghosts, means, d_ref, emit):
    vel_ref, th_ref, me_ref = means
    if ghosts is not None:
        faces, _, _, yg, flat, zg_ref = ghosts
        edge = split3(jnp.concatenate([faces[4], faces[5]], axis=1))
    for n in range(7):
        wide = min(256, PLANE - 256 * n)
        slot = n % 2
        along = [None, None]
        if x_ref is not None:
            ty_ref, tz_ref = tables
            low = max(0, 256 * n - 128)
            high = min(PLANE, 256 * n + 384)
            skip = low - (256 * n - 128)
            size = high - low
            parts = split3(x_ref[block, :, :, pl.ds(low, size)].reshape(ROWS, size))
            ty = ty_ref[pl.ds(skip, size), pl.ds(0, wide)]
            tz = tz_ref[n % 5, pl.ds(skip, size), pl.ds(0, wide)]
            for part in parts:
                along[0] = add(along[0], jnp.dot(part, ty, preferred_element_type=F32))
                along[1] = add(along[1], jnp.dot(part, tz, preferred_element_type=F32))
        if ghosts is not None:
            table = zg_ref[:, pl.ds(256 * n, wide)]
            for part in edge:
                along[1] = add(along[1], jnp.dot(part, table, preferred_element_type=F32))
        for which in range(2):
            if along[which] is not None:
                d_ref[slot, which, :, pl.ds(0, wide)] = along[which]
        for at in range(0, wide, 128):
            w = min(128, wide - at)
            t = 2 * n + at // 128
            lanes = pl.ds(128 * t, w)
            for g in range(5):
                rows = pl.ds(8 * g, 8)
                dx, dy, dz = [], [], []
                for f in range(FIELDS):
                    own_rows = pl.ds(f * W + 8 * g, 8)
                    x = y = None
                    if x_ref is not None:
                        x = inner_first(x_ref, block, f, g, lanes, w)
                        y = d_ref[slot, 0, own_rows, pl.ds(at, w)]
                    if ghosts is not None:
                        if g in (0, 4):
                            x = add(x, ghost_first(flat, f, g, lanes, w))
                        if t in (0, 11, 12):
                            y = add(y, yg[{0: 0, 11: 1, 12: 2}[t], own_rows, pl.ds(0, w)])
                    dx.append(x)
                    dy.append(y)
                    dz.append(d_ref[slot, 1, own_rows, pl.ds(at, w)])
                out = combine(
                    dx if dx[0] is not None else None,
                    dy if dy[0] is not None else None,
                    dz,
                    [vel_ref[block, d, rows, lanes] for d in range(3)],
                    [th_ref[block, d, rows, lanes] for d in range(2)],
                    [me_ref[block, d, rows, lanes] for d in range(3)],
                    scale / 60.0,
                )
                for f in range(FIELDS):
                    emit(f, g, rows, lanes, w, out[f])


def both_blocks(body):
    def step(block, carry):
        body(block)
        return carry

    lax.fori_loop(0, 2, step, 0)


def pack(owner_ref, rows_ref, out_ref, count, wide):
    devices = out_ref.shape[0]
    rows = owner_ref.shape[0]
    sub = iota((8, 128), 0)
    lane = iota((8, 128), 1)
    empty = jnp.where((sub % 4 == 1) & (lane == 127), -1.0, 0.0).astype(F32)
    wide[...] = jnp.zeros_like(wide)
    for s in range(2):
        wide[2 * s] = rows_ref[s, :, pl.ds(0, 128)]
        wide[2 * s + 1, :, pl.ds(0, 72)] = rows_ref[s, :, pl.ds(128, 72)]

    def clear(d, carry):
        count[d] = 0
        out_ref[d] = empty
        return carry

    lax.fori_loop(0, devices, clear, 0, unroll=8)
    lane1 = iota((1, 128), 1)

    def place(i, carry):
        line = owner_ref[i]
        target = lax.shift_right_logical(line * 52429, 22)
        local = (line - target * (2 * W)).astype(F32)
        slot = count[target]
        count[target] = slot + 1
        for s in range(2):
            for j in range(2):
                value = wide[2 * s + j, pl.ds(i, 1), :]
                if s == 0 and j == 1:
                    value = jnp.where(lane1 == 127, local, value)
                out_ref[target, pl.ds(4 * slot + 2 * s + j, 1), :] = value
        return carry

    lax.fori_loop(0, rows, place, 0, unroll=8)


def first_kernel(
    owner_hbm,
    rows_hbm,
    link_hbm,
    kind_hbm,
    x_hbm,
    pick_hbm,
    sent_hbm,
    own_hbm,
    a_hbm,
    b_hbm,
    meta_hbm,
    owner_ref,
    count,
    link_ref,
    kind_ref,
    meta_ref,
    rows_ref,
    wide,
    sent,
    x_ref,
    pick_ref,
    own_ref,
    strips,
    sems,
    own_sems,
    hand_sems,
):
    loads = [
        pltpu.make_async_copy(*pair, sems.at[i])
        for i, pair in enumerate(
            [
                (owner_hbm, owner_ref),
                (rows_hbm, rows_ref),
                (link_hbm, link_ref),
                (kind_hbm, kind_ref),
                (pick_hbm, pick_ref),
                (x_hbm.at[0], x_ref.at[0]),
                (x_hbm.at[1], x_ref.at[1]),
            ]
        )
    ]
    for load in loads:
        load.start()
    for load in loads[:4]:
        load.wait()
    pack(owner_ref, rows_ref, sent, count, wide)
    send = pltpu.make_async_copy(sent, sent_hbm, sems.at[7])
    send.start()
    cycle = lax.axis_size("blk")
    row_start = lax.axis_index("les") * cycle
    column = lax.axis_index("blk")
    above = row_start + lax.rem(column + 1, cycle)
    below = row_start + lax.rem(column + cycle - 1, cycle)
    even = lax.rem(column, 2) == 0
    partner_a = jnp.where(even, above, below)
    partner_b = jnp.where(even, below, above)
    partner, to_a, to_b = [], [], []
    count_a = jnp.int32(0)
    count_b = jnp.int32(0)
    for i in range(12):
        target = link_ref[0, i // 6, i % 6]
        device = lax.shift_right_logical(target, 1)
        linked = kind_ref[i // 6, i % 6] == 0
        is_a = linked & (device == partner_a)
        is_b = linked & (device == partner_b)
        partner.append((target - 2 * device) * 6 + link_ref[1, i // 6, i % 6])
        to_a.append(is_a)
        to_b.append(is_b)
        meta_ref[1, i] = jnp.where(is_a, 1 + count_a, jnp.where(is_b, 1 + FACE_CAP + count_b, 0))
        count_a = count_a + is_a.astype(jnp.int32)
        count_b = count_b + is_b.astype(jnp.int32)
    for i in range(12):
        rank_a = jnp.int32(0)
        rank_b = jnp.int32(0)
        for j in range(12):
            less = partner[j] < partner[i]
            rank_a = rank_a + (to_a[j] & less).astype(jnp.int32)
            rank_b = rank_b + (to_b[j] & less).astype(jnp.int32)
        meta_ref[0, i] = jnp.where(
            to_a[i], 12 + rank_a, jnp.where(to_b[i], 12 + FACE_CAP + rank_b, partner[i])
        )
    meta_out = pltpu.make_async_copy(meta_ref, meta_hbm, sems.at[8])
    meta_out.start()
    for load in loads[4:]:
        load.wait()

    def copies(face):
        place = meta_ref[1, face]
        return (
            (place >= 1) & (place < 1 + FACE_CAP),
            lambda: pltpu.make_async_copy(
                own_ref.at[face], a_hbm.at[place - 1], hand_sems.at[face]
            ),
            place >= 1 + FACE_CAP,
            lambda: pltpu.make_async_copy(
                own_ref.at[face], b_hbm.at[place - 1 - FACE_CAP], hand_sems.at[face]
            ),
        )

    def keep(block):
        return pltpu.make_async_copy(
            own_ref.at[pl.ds(6 * block, 6)], own_hbm.at[pl.ds(6 * block, 6)], own_sems.at[block]
        )

    def body(block):
        extract(x_ref, block, pick_ref, own_ref, strips)
        for i in range(6):
            is_a, copy_a, is_b, copy_b = copies(6 * block + i)

            @pl.when(is_a)
            def _():
                copy_a().start()

            @pl.when(is_b)
            def _():
                copy_b().start()

        keep(block).start()

    both_blocks(body)
    for face in range(12):
        is_a, copy_a, is_b, copy_b = copies(face)

        @pl.when(is_a)
        def _():
            copy_a().wait()

        @pl.when(is_b)
        def _():
            copy_b().wait()

    for block in range(2):
        keep(block).wait()
    send.wait()
    meta_out.wait()


def load_all(pairs, sems):
    loads = [pltpu.make_async_copy(*pair, sems.at[i]) for i, pair in enumerate(pairs)]
    for load in loads:
        load.start()
    return loads


def inner_kernel(scale, *refs):
    sources = refs[:6]
    part, vel, th, me = refs[6:10]
    ty, tz, x_ref, d_ref, sems = refs[10:15]
    pairs = [[(sources[0], ty), (sources[1], tz)], []]
    for block in range(2):
        for source, target in zip(sources[2:], (x_ref, vel, th, me)):
            pairs[block].append((source.at[block], target.at[block]))
    loads = load_all(pairs[0] + pairs[1], sems)

    def body(block):
        @pl.when(block == 0)
        def _():
            for load in loads[:6]:
                load.wait()

        @pl.when(block == 1)
        def _():
            for load in loads[6:]:
                load.wait()

        def emit(f, g, rows, lanes, w, value):
            part[block, f, rows, lanes] = -value

        sweep(block, scale, x_ref, (ty, tz), None, (vel, th, me), d_ref, emit)

    both_blocks(body)


def inject(got_ref, src, strips):
    rows = got_ref.shape[0] // 4
    lane = iota((rows, 128), 1)
    parts = [got_ref[pl.ds(j, rows, stride=4), :] for j in range(4)]
    label = jnp.max(jnp.where(lane == 127, parts[1], -1.0), axis=1, keepdims=True)
    chosen = jnp.where(label == lane.astype(F32), 1.0, 0.0)
    chooser = jnp.transpose(chosen).astype(BF16)
    lane = iota((W, 128), 1)
    lane8 = iota((8, 128), 1)
    for s in range(2):
        sums = []
        for j in range(2):
            total = None
            for part in split3(parts[2 * s + j]):
                total = add(total, jnp.dot(chooser, part, preferred_element_type=F32))
            sums.append(total)
        for b in range(2):
            left, right = (value[b * W : b * W + W] for value in sums)
            for f in range(FIELDS):
                if f < 3:
                    piece = left
                elif f == 3:
                    piece = jnp.where(lane >= 120, left, right)
                else:
                    piece = right
                strips[pl.ds(f, W, stride=8), :] = roll_lanes(piece, -W * f)
            for t in range(TILES):
                total = None
                for y in range(W):
                    start = W * y - 128 * t
                    if start + W <= 0 or start >= 128:
                        continue
                    value = roll_lanes(strips[pl.ds(y * 8, 8), :], start)
                    total = value if total is None else jnp.where(lane8 >= start, value, total)
                src[s, b, :, pl.ds(128 * t, 128)] = total


def middle_kernel(scale, *refs):
    sources, got, outs = refs[:4], refs[4], refs[5:11]
    section, mid, own, a, b, src = outs
    held, strips, lines, sems = refs[11:15], refs[15], refs[16], refs[17]
    loads = load_all(zip(sources, held), sems)
    meta, pre, q_ref, pick = held
    inject(got, src, lines)
    for load in loads:
        load.wait()

    def body(block):
        for f in range(FIELDS):
            value = pre[block, f]
            line = scale * src[0, block, pl.ds(f, 1), pl.ds(0, PLANE)]
            top = value[:8]
            top = jnp.where(iota((8, PLANE), 0) == 0, top + line, top)
            section[block, f, pl.ds(0, 8), :] = top
            section[block, f, pl.ds(8, W - 8), :] = value[8:]
            mid[block, f, pl.ds(0, 8), :] = q_ref[block, f, pl.ds(0, 8), :] + top
            mid[block, f, pl.ds(8, W - 8), :] = q_ref[block, f, pl.ds(8, W - 8), :] + value[8:]
        extract(mid, block, pick, own, strips)

    both_blocks(body)
    hand_out(own, a, b, meta)


def early_kernel(meta, link, kind, own, a, faces, swapped):
    for face in range(12):
        source = meta[0, face]

        @pl.when(source < 12 + FACE_CAP)
        def _():
            keep = jnp.where(kind[face // 6, face % 6] == 2, 0.0, 1.0).astype(F32)
            code = link[2, face // 6, face % 6]
            turn_face(own, a, None, source, code, keep, faces, face, swapped.at[face % 6])


def interior_kernel(scale, x_ref, section, vel, th, me, ty, tz, part, out_hbm, d_ref, sem):
    copy = pltpu.make_async_copy(section, out_hbm, sem)
    copy.start()

    def body(block):
        def emit(f, g, rows, lanes, w, value):
            part[block, f, rows, lanes] = -value

        sweep(block, scale, x_ref, (ty, tz), None, (vel, th, me), d_ref, emit)

    both_blocks(body)
    copy.wait()


def ghost_kernel(scale, last, *refs):
    meta, link, kind = refs[:3]
    own, a, b = (None, None, refs[4]) if last else refs[3:6]
    early = refs[3] if last else None
    refs = refs[5 if last else 6 :]
    part, vel, th, me, zg = refs[:5]
    src = refs[5] if last else None
    refs = refs[5 + last :]
    out_hbm, ghost, d_ref, out, sems = refs[0], refs[1:6], refs[6], refs[7], refs[8]

    def copy(block):
        return pltpu.make_async_copy(out.at[block], out_hbm.at[block], sems.at[block])

    def body(block):
        prepare_ghosts(block, meta, link, kind, own, a, b, ghost, early)

        def emit(f, g, rows, lanes, w, value):
            value = part[block, f, rows, lanes] - value
            if last and g == 0:
                line = scale * src[1, block, pl.ds(f, 1), lanes]
                value = jnp.where(iota((8, w), 0) == 0, value + line, value)
            out[block, f, rows, lanes] = value

        sweep(block, scale, None, None, tuple(ghost) + (zg,), (vel, th, me), d_ref, emit)
        copy(block).start()

    both_blocks(body)
    for block in range(2):
        copy(block).wait()


SMEM = pl.BlockSpec(memory_space=pltpu.SMEM)
VMEM = pl.BlockSpec(memory_space=pltpu.VMEM)
ANY = pl.BlockSpec(memory_space=pl.ANY)


def near(x):
    return pltpu.with_memory_space_constraint(x, pltpu.VMEM)


def far(x):
    return pltpu.with_memory_space_constraint(x, pltpu.HBM)


def cost(flops, size):
    return pl.CostEstimate(flops=flops, bytes_accessed=size, transcendentals=0)


def call(kernel, name, arrays, outs, scratch, flops=0, size=10**6, smem=(), remote=()):
    specs = [VMEM if spot is None else spot for spot, _ in outs]
    return pl.pallas_call(
        kernel,
        in_specs=[SMEM] * len(smem) + [ANY] * len(remote) + [VMEM] * len(arrays),
        out_specs=specs,
        out_shape=[shape for _, shape in outs],
        scratch_shapes=scratch,
        compiler_params=pltpu.CompilerParams(vmem_limit_bytes=VMEM_LIMIT),
        cost_estimate=cost(flops, size),
        name=name,
    )(*smem, *[far(x) for x in remote], *[near(x) for x in arrays])


def held_in(x, kind=pltpu.VMEM):
    return kind(x.shape, x.dtype)


def out_far(shape, dtype=F32):
    return (ANY, pltpu.HBM(shape, dtype))


def out_near(shape):
    return (None, pltpu.VMEM(shape, F32))


VOLUME = (2, FIELDS, W, PLANE)
FACE = (ROWS, 128)


def exchange(a, b):
    n = lax.axis_size("blk")
    odd = [(i, (i + 1) % n) for i in range(1, n, 2)]
    b = lax.ppermute(b, "blk", odd + [(j, i) for i, j in odd])
    return lax.ppermute(a, "blk", [(i, i ^ 1) for i in range(n)]), b


def local(field, velocity, thermo, metric, inlet_rows, row_owner, face_link, face_kind):
    devices = lax.axis_size("les") * lax.axis_size("blk")
    ty = jnp.asarray(second_table(), BF16)
    tz = jnp.asarray(third_tables(), BF16)
    zg = jnp.asarray(third_ghost_table(), BF16)
    pick = jnp.asarray(third_pick_table(), BF16)
    c1, c2 = (TIME_STEP * w for w in SECTION_WEIGHTS)
    link = jnp.transpose(face_link, (2, 0, 1))
    means = [velocity, thermo, metric]
    d_scratch = pltpu.VMEM((2, 2, ROWS, 256), F32)
    strips = pltpu.VMEM((W * W, 128), F32)
    volume = pltpu.VMEM(VOLUME, F32)
    counts = [12, FACE_CAP, FACE_CAP]
    dma = pltpu.SemaphoreType.DMA

    inputs = [row_owner, inlet_rows, link, face_kind, field, pick]
    sent, own, a, b, meta = call(
        first_kernel,
        "first_faces",
        [],
        [out_far((devices, 8, 128))]
        + [out_far((n,) + FACE) for n in counts]
        + [out_far((2, 12), jnp.int32)],
        [
            held_in(row_owner, pltpu.SMEM),
            pltpu.SMEM((devices,), jnp.int32),
            held_in(link, pltpu.SMEM),
            held_in(face_kind, pltpu.SMEM),
            pltpu.SMEM((2, 12), jnp.int32),
            held_in(inlet_rows),
            pltpu.VMEM((4, inlet_rows.shape[1], 128), F32),
            pltpu.VMEM((devices, 8, 128), F32),
            volume,
            held_in(pick),
            pltpu.VMEM((12,) + FACE, F32),
            strips,
            dma((9,)),
            dma((2,)),
            dma((12,)),
        ],
        10**9,
        remote=inputs,
    )
    a, b = exchange(a, b)
    got = lax.all_to_all(sent, ("les", "blk"), split_axis=0, concat_axis=0, tiled=True)
    scalars = [meta, link, face_kind]
    ghost_scratch = GHOST_SCRATCH + [d_scratch, volume, dma((2,))]
    part, *means = call(
        functools.partial(inner_kernel, c1),
        "inner_first",
        [],
        [out_near(x.shape) for x in [field] + means],
        [held_in(ty), held_in(tz), volume, d_scratch, dma((10,))],
        100000000,
        1000000,
        remote=[ty, tz, field] + means,
    )
    (pre,) = call(
        functools.partial(ghost_kernel, c1, False),
        "ghosts_first",
        [own, a, b, part] + means + [zg],
        [out_far(VOLUME)],
        ghost_scratch,
        2000000000,
        1000000,
        smem=scalars,
    )
    got = got.reshape(devices * 8, 128)
    inputs = [meta, pre, field, pick]
    section, middle, own, a, b, src = call(
        functools.partial(middle_kernel, c1),
        "middle_faces",
        [got],
        [out_near(VOLUME), out_near(VOLUME)]
        + [out_near((n,) + FACE) for n in counts]
        + [out_near((2, 2, 8, 128 * TILES))],
        [held_in(meta, pltpu.SMEM)]
        + [held_in(x) for x in inputs[1:]]
        + [strips, pltpu.VMEM((W * 8, 128), F32), dma((4,))],
        2 * 10**9,
        6 * 10**6,
        remote=inputs,
    )
    means = [velocity, thermo, metric]
    a, b = exchange(a, b)
    part, first = call(
        functools.partial(interior_kernel, c2),
        "interior",
        [middle, section] + means + [ty, tz],
        [out_near(VOLUME), out_far(VOLUME)],
        [d_scratch, dma],
        6 * 10**9,
        12 * 10**6,
    )
    (early,) = call(
        early_kernel,
        "turn_early",
        [own, a],
        [out_near((12,) + FACE)],
        [pltpu.VMEM((6,) + FACE, F32)],
        10**8,
        10**6,
        smem=scalars,
    )
    (second,) = call(
        functools.partial(ghost_kernel, c2, True),
        "ghosts_last",
        [early, b, part] + means + [zg, src],
        [out_far(VOLUME)],
        ghost_scratch,
        2 * 10**9,
        smem=scalars,
    )
    return first, second


def solution(mesh):
    both = ("les", "blk")
    return jax.shard_map(
        local,
        mesh=mesh,
        in_specs=(
            P(both, None, None, None),
            P(both, None, None, None),
            P(both, None, None, None),
            P(both, None, None, None),
            P(None, both, None),
            P(both),
            P(both, None, None),
            P(both, None),
        ),
        out_specs=(P(both, None, None, None), P(both, None, None, None)),
        check_vma=False,
    )
```

```python
import functools

import jax
import jax.numpy as jnp
import numpy as np
from jax import lax
from jax.experimental import pallas as pl
from jax.experimental.pallas import tpu as pltpu
from jax.sharding import PartitionSpec as P

CAP = 2
FACE_CAP = 4
W = 40
PLANE = W * W
FIELDS = 5
ROWS = FIELDS * W
TILES = 13
INTS = (45.0, -9.0, 1.0)
GAMMA_GAS = 1.4
TIME_STEP = 0.5
SECTION_WEIGHTS = (0.117979901, 0.184646966)
VMEM_LIMIT = 28 * 1024 * 1024
F32 = jnp.float32
BF16 = jnp.bfloat16


def weight_of(offset):
    total = np.zeros(offset.shape, np.float32)
    for step in range(3):
        total += INTS[step] * ((offset == step + 1).astype(np.float32) - (offset == -step - 1))
    return total


def second_table():
    k = np.arange(512)[:, None] - 128
    lane = np.arange(256)[None, :]
    gap = k - lane
    return weight_of(np.where(gap % W == 0, gap // W, 99))


def third_tables():
    tables = []
    for n in range(5):
        k = np.arange(512)[:, None] - 128 + 256 * n
        lane = np.arange(256)[None, :] + 256 * n
        same = (k // W) == (lane // W)
        tables.append(weight_of(np.where(same, k - lane, 99)))
    return np.stack(tables)


def third_ghost_table():
    lane = np.arange(PLANE)[None, :]
    out = np.zeros((256, PLANE), np.float32)
    edge = np.arange(3 * W)[:, None]
    depth, across = edge // W, edge % W
    match = across == lane // W
    out[: 3 * W] = match * weight_of(-1 - depth - lane % W)
    out[128 : 128 + 3 * W] = match * weight_of(W + depth - lane % W)
    return out


def third_pick_table():
    lane = np.arange(PLANE)[:, None]
    out = np.zeros((PLANE, 256), np.float32)
    edge = np.arange(3 * W)[None, :]
    depth, across = edge // W, edge % W
    match = across == lane // W
    out[:, : 3 * W] = match & (lane % W == depth)
    out[:, 128 : 128 + 3 * W] = match & (lane % W == W - 1 - depth)
    return out


def iota(shape, dim):
    return lax.broadcasted_iota(jnp.int32, shape, dim)


def split3(x):
    high = x.astype(BF16)
    rest = x - high.astype(F32)
    mid = rest.astype(BF16)
    low = (rest - mid.astype(F32)).astype(BF16)
    return high, mid, low


def product3(x, table):
    total = None
    for part in split3(x):
        term = jnp.dot(part, table, preferred_element_type=F32)
        total = term if total is None else total + term
    return total


def roll_lanes(x, by):
    by = by % 128
    return x if by == 0 else pltpu.roll(x, by, x.ndim - 1)


def lane_tile(ref, lead, rows, t):
    if t < 12:
        return ref[lead + (rows, pl.ds(128 * t, 128))]
    part = ref[lead + (rows, pl.ds(1536, 64))]
    return jnp.concatenate([part, jnp.zeros(part.shape[:-1] + (64,), F32)], axis=-1)


def combine(dx, dy, dz, velocity, thermo, metric, scale):
    density, pressure = thermo
    carried = [None] * FIELDS
    spread = None
    inverse = 1.0 / density
    extra = {}
    for d, grad in enumerate((dx, dy, dz)):
        if grad is None:
            continue
        m = metric[d] * scale
        a = velocity[d] * m
        for f in range(FIELDS):
            term = a * grad[f]
            carried[f] = term if carried[f] is None else carried[f] + term
        term = m * grad[1 + d]
        spread = term if spread is None else spread + term
        extra[1 + d] = (m * inverse) * grad[4]
    out = [carried[0] + density * spread]
    for f in (1, 2, 3):
        out.append(carried[f] + extra[f] if f in extra else carried[f])
    out.append(carried[4] + (GAMMA_GAS * pressure) * spread)
    return out


def extract(x_ref, block, pick_ref, own_ref, strips):
    base = 6 * block
    lane = iota((W, 128), 1)
    for f in range(FIELDS):
        rows = pl.ds(f * W, W)
        own_ref[base + 2, rows, :] = x_ref[block, f, :, pl.ds(0, 128)]
        b = lane_tile(x_ref, (block, f), pl.ds(0, W), 11)
        a = lane_tile(x_ref, (block, f), pl.ds(0, W), 12)
        middle = jnp.where(lane < 56, roll_lanes(b, 56), roll_lanes(a, 56))
        own_ref[base + 3, rows, :] = jnp.where(
            lane < 40, roll_lanes(a, -24), jnp.where(lane < 80, middle, roll_lanes(b, 8))
        )
    picked = product3(x_ref[block].reshape(ROWS, PLANE), pick_ref[...])
    own_ref[base + 4] = picked[:, :128]
    own_ref[base + 5] = picked[:, 128:]
    sub = iota((8, 128), 0)
    lane8 = iota((8, 128), 1)
    for t in range(TILES):
        for f in range(FIELDS):
            low = lane_tile(x_ref, (block, f), pl.ds(0, 8), t)
            high = lane_tile(x_ref, (block, f), pl.ds(32, 8), t)
            both = jnp.where(sub < 4, low, high)
            for y in range(W):
                start = W * y - 128 * t
                if start >= 0 and start < 128:
                    value = roll_lanes(both, -start)
                    strips[pl.ds(y * W + f * 8, 8), :] = value
                elif start < 0 and start + W > 0:
                    value = roll_lanes(both, -start)
                    old = strips[pl.ds(y * W + f * 8, 8), :]
                    strips[pl.ds(y * W + f * 8, 8), :] = jnp.where(lane8 < -start, old, value)
    for f in range(FIELDS):
        rows = pl.ds(f * W, W)
        for side in range(2):
            parts = []
            for k in range(3):
                row = f * 8 + (7 - k if side else k)
                parts.append(roll_lanes(strips[pl.ds(row, W, stride=W), :], W * k))
            own_ref[base + side, rows, :] = jnp.where(
                lane < 40, parts[0], jnp.where(lane < 80, parts[1], parts[2])
            )


def hand_out(own_ref, a_ref, b_ref, meta_ref):
    for face in range(12):
        place = meta_ref[1, face]

        @pl.when((place >= 1) & (place < 1 + FACE_CAP))
        def _():
            a_ref[place - 1] = own_ref[face]

        @pl.when(place >= 1 + FACE_CAP)
        def _():
            b_ref[place - 1 - FACE_CAP] = own_ref[face]


def flatten_strips(strips, write):
    lane = iota((W, 128), 1)
    for t in range(TILES):
        total = None
        for y in range(W):
            start = W * y - 128 * t
            if start + W <= 0 or start >= 128:
                continue
            value = roll_lanes(strips[pl.ds(y * W, W), :], start)
            if total is None:
                total = value
            else:
                total = jnp.where(lane >= start, value, total)
        write(t, total)


def second_ghosts(face_low, face_high, yg):
    lane = iota((W, 128), 1)

    def near(face):
        first = INTS[0] * face + INTS[1] * roll_lanes(face, -40) + INTS[2] * roll_lanes(face, -80)
        second = INTS[1] * roll_lanes(face, 40) + INTS[2] * face
        third = INTS[2] * roll_lanes(face, 80)
        return jnp.where(
            lane < 40,
            first,
            jnp.where(lane < 80, second, jnp.where(lane < 120, third, jnp.zeros_like(face))),
        )

    for f in range(FIELDS):
        rows = pl.ds(f * W, W)
        yg[0, rows, :] = -near(face_low(rows))
        value = near(face_high(rows))
        crossing = roll_lanes(value, -56)
        zero = jnp.zeros_like(value)
        yg[1, rows, :] = jnp.where(
            lane >= 112, crossing, jnp.where(lane >= 72, roll_lanes(value, -8), zero)
        )
        yg[2, rows, :] = jnp.where(
            lane < 24, crossing, jnp.where(lane < 64, roll_lanes(value, 24), zero)
        )


def turn_face(own_ref, a_ref, b_ref, source, code, keep, faces, slot, swapped):
    if own_ref is None:
        swapped[...] = b_ref[source - 12 - FACE_CAP]
    else:

        @pl.when(source < 12)
        def _():
            swapped[...] = own_ref[source]

        @pl.when((source >= 12) & (source < 12 + FACE_CAP))
        def _():
            swapped[...] = a_ref[source - 12]

        if b_ref is not None:

            @pl.when(source >= 12 + FACE_CAP)
            def _():
                swapped[...] = b_ref[source - 12 - FACE_CAP]

    @pl.when(code >= 4)
    def _():
        lane = iota((W, 128), 1)
        whole = jnp.concatenate([swapped[...], jnp.zeros((56, 128), F32)], axis=0)
        left = jnp.transpose(whole[:128])
        right = jnp.transpose(whole[128:])
        for f in range(FIELDS):
            parts = []
            for k in range(3):
                rows = slice(k * W, k * W + W)
                shift = W * k - W * f
                if f < 3:
                    piece = left[rows]
                elif f == 3:
                    piece = jnp.where(lane >= 120, left[rows], right[rows])
                else:
                    piece = right[rows]
                parts.append(roll_lanes(piece, shift))
            swapped[pl.ds(f * W, W), :] = jnp.where(
                lane < 40, parts[0], jnp.where(lane < 80, parts[1], parts[2])
            )

    flip_a = code % 2
    flip_b = (code // 2) % 2
    lane = iota((8, 128), 1)
    depth = (lane >= 40).astype(jnp.int32) + (lane >= 80).astype(jnp.int32)
    mirrored = jnp.where(lane < 120, 2 * W * depth + (W - 1) - lane, lane)
    lane_index = jnp.where(flip_b == 1, mirrored, lane)
    sub = iota((8, 128), 0)
    sub_index = jnp.where(flip_a == 1, 7 - sub, sub)
    for f in range(FIELDS):
        for g in range(5):
            start = f * W + 8 * jnp.where(flip_a == 1, 4 - g, g)
            value = swapped[pl.ds(pl.multiple_of(start, 8), 8), :]
            value = jnp.take_along_axis(value, lane_index, axis=1, mode="promise_in_bounds")
            value = jnp.take_along_axis(value, sub_index, axis=0, mode="promise_in_bounds")
            faces[slot, pl.ds(f * W + 8 * g, 8), :] = value * keep


def prepare_ghosts(
    block, meta_ref, link_ref, kind_ref, own_ref, a_ref, b_ref, scratch, early=None
):
    faces, swapped, strips, yg, flat = scratch
    for face in range(6):
        index = block * 6 + face
        source = meta_ref[0, index]

        def turn():
            keep = jnp.where(kind_ref[block, face] == 2, 0.0, 1.0).astype(F32)
            code = link_ref[2, block, face]
            turn_face(own_ref, a_ref, b_ref, source, code, keep, faces, face, swapped.at[face])

        if early is None:
            turn()
        else:
            pl.when(source >= 12 + FACE_CAP)(turn)

            @pl.when(source < 12 + FACE_CAP)
            def _():
                faces[face] = early[index]

    second_ghosts(lambda rows: faces[2, rows, :], lambda rows: faces[3, rows, :], yg)
    for f in range(FIELDS):
        for side in range(2):
            value = faces[side, pl.ds(f * W, W), :]
            for k in range(3):
                row = f * 8 + (7 - k if side else k)
                strips[pl.ds(row, W, stride=W), :] = roll_lanes(value, -W * k)

    def write(t, value):
        flat[:, pl.ds(128 * t, 128)] = value

    flatten_strips(strips, write)


GHOST_SCRATCH = [
    pltpu.VMEM((6, ROWS, 128), F32),
    pltpu.VMEM((6, ROWS, 128), F32),
    pltpu.VMEM((W * W, 128), F32),
    pltpu.VMEM((3, ROWS, 128), F32),
    pltpu.VMEM((W, 128 * TILES), F32),
]


def add(a, b):
    return b if a is None else a + b


def inner_first(x_ref, block, f, g, lanes, w):
    sub = iota((8, w), 0)
    cur = x_ref[block, f, pl.ds(8 * g, 8), lanes]
    zero = jnp.zeros_like(cur)
    before = x_ref[block, f, pl.ds(8 * g - 8, 8), lanes] if g > 0 else zero
    after = x_ref[block, f, pl.ds(8 * g + 8, 8), lanes] if g < 4 else zero
    total = None
    for j in (1, 2, 3):
        plus = pltpu.roll(jnp.where(sub >= j, cur, after), 8 - j, 0)
        minus = pltpu.roll(jnp.where(sub < 8 - j, cur, before), j, 0)
        total = add(total, INTS[j - 1] * (plus - minus))
    return total


def ghost_first(flat, f, g, lanes, w):
    sub = iota((8, w), 0)
    ghost = [flat[pl.ds(f * 8 + (7 - k if g else k), 1), lanes] for k in range(3)]
    far = (7 - sub) if g else sub
    total = jnp.zeros((8, w), F32)
    for m in range(3):
        row = None
        for k in range(3 - m):
            row = add(row, INTS[m + k] * ghost[k])
        total = jnp.where(far == m, row, total)
    return total if g else -total


def sweep(block, scale, x_ref, tables, ghosts, means, d_ref, emit):
    vel_ref, th_ref, me_ref = means
    if ghosts is not None:
        faces, _, _, yg, flat, zg_ref = ghosts
        edge = split3(jnp.concatenate([faces[4], faces[5]], axis=1))
    for n in range(7):
        wide = min(256, PLANE - 256 * n)
        slot = n % 2
        along = [None, None]
        if x_ref is not None:
            ty_ref, tz_ref = tables
            low = max(0, 256 * n - 128)
            high = min(PLANE, 256 * n + 384)
            skip = low - (256 * n - 128)
            size = high - low
            parts = split3(x_ref[block, :, :, pl.ds(low, size)].reshape(ROWS, size))
            ty = ty_ref[pl.ds(skip, size), pl.ds(0, wide)]
            tz = tz_ref[n % 5, pl.ds(skip, size), pl.ds(0, wide)]
            for part in parts:
                along[0] = add(along[0], jnp.dot(part, ty, preferred_element_type=F32))
                along[1] = add(along[1], jnp.dot(part, tz, preferred_element_type=F32))
        if ghosts is not None:
            table = zg_ref[:, pl.ds(256 * n, wide)]
            for part in edge:
                along[1] = add(along[1], jnp.dot(part, table, preferred_element_type=F32))
        for which in range(2):
            if along[which] is not None:
                d_ref[slot, which, :, pl.ds(0, wide)] = along[which]
        for at in range(0, wide, 128):
            w = min(128, wide - at)
            t = 2 * n + at // 128
            lanes = pl.ds(128 * t, w)
            for g in range(5):
                rows = pl.ds(8 * g, 8)
                dx, dy, dz = [], [], []
                for f in range(FIELDS):
                    own_rows = pl.ds(f * W + 8 * g, 8)
                    x = y = None
                    if x_ref is not None:
                        x = inner_first(x_ref, block, f, g, lanes, w)
                        y = d_ref[slot, 0, own_rows, pl.ds(at, w)]
                    if ghosts is not None:
                        if g in (0, 4):
                            x = add(x, ghost_first(flat, f, g, lanes, w))
                        if t in (0, 11, 12):
                            y = add(y, yg[{0: 0, 11: 1, 12: 2}[t], own_rows, pl.ds(0, w)])
                    dx.append(x)
                    dy.append(y)
                    dz.append(d_ref[slot, 1, own_rows, pl.ds(at, w)])
                out = combine(
                    dx if dx[0] is not None else None,
                    dy if dy[0] is not None else None,
                    dz,
                    [vel_ref[block, d, rows, lanes] for d in range(3)],
                    [th_ref[block, d, rows, lanes] for d in range(2)],
                    [me_ref[block, d, rows, lanes] for d in range(3)],
                    scale / 60.0,
                )
                for f in range(FIELDS):
                    emit(f, g, rows, lanes, w, out[f])


def both_blocks(body):
    def step(block, carry):
        body(block)
        return carry

    lax.fori_loop(0, 2, step, 0)


def pack(owner_ref, rows_ref, out_ref, count, wide):
    devices = out_ref.shape[0]
    rows = owner_ref.shape[0]
    sub = iota((8, 128), 0)
    lane = iota((8, 128), 1)
    empty = jnp.where((sub % 4 == 1) & (lane == 127), -1.0, 0.0).astype(F32)
    wide[...] = jnp.zeros_like(wide)
    for s in range(2):
        wide[2 * s] = rows_ref[s, :, pl.ds(0, 128)]
        wide[2 * s + 1, :, pl.ds(0, 72)] = rows_ref[s, :, pl.ds(128, 72)]

    def clear(d, carry):
        count[d] = 0
        out_ref[d] = empty
        return carry

    lax.fori_loop(0, devices, clear, 0, unroll=8)
    lane1 = iota((1, 128), 1)

    def place(i, carry):
        line = owner_ref[i]
        target = lax.shift_right_logical(line * 52429, 22)
        local = (line - target * (2 * W)).astype(F32)
        slot = count[target]
        count[target] = slot + 1
        for s in range(2):
            for j in range(2):
                value = wide[2 * s + j, pl.ds(i, 1), :]
                if s == 0 and j == 1:
                    value = jnp.where(lane1 == 127, local, value)
                out_ref[target, pl.ds(4 * slot + 2 * s + j, 1), :] = value
        return carry

    lax.fori_loop(0, rows, place, 0, unroll=8)


def first_kernel(
    owner_hbm,
    rows_hbm,
    link_hbm,
    kind_hbm,
    x_hbm,
    pick_hbm,
    sent_hbm,
    own_hbm,
    a_hbm,
    b_hbm,
    meta_hbm,
    owner_ref,
    count,
    link_ref,
    kind_ref,
    meta_ref,
    rows_ref,
    wide,
    sent,
    x_ref,
    pick_ref,
    own_ref,
    strips,
    sems,
    own_sems,
    hand_sems,
):
    loads = [
        pltpu.make_async_copy(*pair, sems.at[i])
        for i, pair in enumerate(
            [
                (owner_hbm, owner_ref),
                (rows_hbm, rows_ref),
                (link_hbm, link_ref),
                (kind_hbm, kind_ref),
                (pick_hbm, pick_ref),
                (x_hbm.at[0], x_ref.at[0]),
                (x_hbm.at[1], x_ref.at[1]),
            ]
        )
    ]
    for load in loads:
        load.start()
    for load in loads[:4]:
        load.wait()
    pack(owner_ref, rows_ref, sent, count, wide)
    send = pltpu.make_async_copy(sent, sent_hbm, sems.at[7])
    send.start()
    cycle = lax.axis_size("blk")
    row_start = lax.axis_index("les") * cycle
    column = lax.axis_index("blk")
    above = row_start + lax.rem(column + 1, cycle)
    below = row_start + lax.rem(column + cycle - 1, cycle)
    even = lax.rem(column, 2) == 0
    partner_a = jnp.where(even, above, below)
    partner_b = jnp.where(even, below, above)
    partner, to_a, to_b = [], [], []
    count_a = jnp.int32(0)
    count_b = jnp.int32(0)
    for i in range(12):
        target = link_ref[0, i // 6, i % 6]
        device = lax.shift_right_logical(target, 1)
        linked = kind_ref[i // 6, i % 6] == 0
        is_a = linked & (device == partner_a)
        is_b = linked & (device == partner_b)
        partner.append((target - 2 * device) * 6 + link_ref[1, i // 6, i % 6])
        to_a.append(is_a)
        to_b.append(is_b)
        meta_ref[1, i] = jnp.where(is_a, 1 + count_a, jnp.where(is_b, 1 + FACE_CAP + count_b, 0))
        count_a = count_a + is_a.astype(jnp.int32)
        count_b = count_b + is_b.astype(jnp.int32)
    for i in range(12):
        rank_a = jnp.int32(0)
        rank_b = jnp.int32(0)
        for j in range(12):
            less = partner[j] < partner[i]
            rank_a = rank_a + (to_a[j] & less).astype(jnp.int32)
            rank_b = rank_b + (to_b[j] & less).astype(jnp.int32)
        meta_ref[0, i] = jnp.where(
            to_a[i], 12 + rank_a, jnp.where(to_b[i], 12 + FACE_CAP + rank_b, partner[i])
        )
    meta_out = pltpu.make_async_copy(meta_ref, meta_hbm, sems.at[8])
    meta_out.start()
    for load in loads[4:]:
        load.wait()

    def copies(face):
        place = meta_ref[1, face]
        return (
            (place >= 1) & (place < 1 + FACE_CAP),
            lambda: pltpu.make_async_copy(
                own_ref.at[face], a_hbm.at[place - 1], hand_sems.at[face]
            ),
            place >= 1 + FACE_CAP,
            lambda: pltpu.make_async_copy(
                own_ref.at[face], b_hbm.at[place - 1 - FACE_CAP], hand_sems.at[face]
            ),
        )

    def keep(block):
        return pltpu.make_async_copy(
            own_ref.at[pl.ds(6 * block, 6)], own_hbm.at[pl.ds(6 * block, 6)], own_sems.at[block]
        )

    def body(block):
        extract(x_ref, block, pick_ref, own_ref, strips)
        for i in range(6):
            is_a, copy_a, is_b, copy_b = copies(6 * block + i)

            @pl.when(is_a)
            def _():
                copy_a().start()

            @pl.when(is_b)
            def _():
                copy_b().start()

        keep(block).start()

    both_blocks(body)
    for face in range(12):
        is_a, copy_a, is_b, copy_b = copies(face)

        @pl.when(is_a)
        def _():
            copy_a().wait()

        @pl.when(is_b)
        def _():
            copy_b().wait()

    for block in range(2):
        keep(block).wait()
    send.wait()
    meta_out.wait()


def loads_of(pairs, sems):
    return [pltpu.make_async_copy(*pair, sems.at[i]) for i, pair in enumerate(pairs)]


def start_all(loads):
    for load in loads:
        load.start()


def wait_all(loads):
    for load in loads:
        load.wait()


def inner_kernel(scale, *refs):
    sources = refs[:6]
    part, vel, th, me = refs[6:10]
    ty, tz, x_ref, d_ref, sems = refs[10:15]
    pairs = [[(sources[0], ty), (sources[1], tz)], []]
    for block in range(2):
        for source, target in zip(sources[2:], (x_ref, vel, th, me)):
            pairs[block].append((source.at[block], target.at[block]))
    loads = loads_of(pairs[0] + pairs[1], sems)
    start_all(loads[:6])

    def body(block):
        @pl.when(block == 0)
        def _():
            wait_all(loads[:6])
            start_all(loads[6:])

        @pl.when(block == 1)
        def _():
            wait_all(loads[6:])

        def emit(f, g, rows, lanes, w, value):
            part[block, f, rows, lanes] = -value

        sweep(block, scale, x_ref, (ty, tz), None, (vel, th, me), d_ref, emit)

    both_blocks(body)


def inject(got_ref, src, strips):
    rows = got_ref.shape[0] // 4
    lane = iota((rows, 128), 1)
    parts = [got_ref[pl.ds(j, rows, stride=4), :] for j in range(4)]
    label = jnp.max(jnp.where(lane == 127, parts[1], -1.0), axis=1, keepdims=True)
    chosen = jnp.where(label == lane.astype(F32), 1.0, 0.0)
    chooser = jnp.transpose(chosen).astype(BF16)
    lane = iota((W, 128), 1)
    lane8 = iota((8, 128), 1)
    for s in range(2):
        sums = []
        for j in range(2):
            total = None
            for part in split3(parts[2 * s + j]):
                total = add(total, jnp.dot(chooser, part, preferred_element_type=F32))
            sums.append(total)
        for b in range(2):
            left, right = (value[b * W : b * W + W] for value in sums)
            for f in range(FIELDS):
                if f < 3:
                    piece = left
                elif f == 3:
                    piece = jnp.where(lane >= 120, left, right)
                else:
                    piece = right
                strips[pl.ds(f, W, stride=8), :] = roll_lanes(piece, -W * f)
            for t in range(TILES):
                total = None
                for y in range(W):
                    start = W * y - 128 * t
                    if start + W <= 0 or start >= 128:
                        continue
                    value = roll_lanes(strips[pl.ds(y * 8, 8), :], start)
                    total = value if total is None else jnp.where(lane8 >= start, value, total)
                src[s, b, :, pl.ds(128 * t, 128)] = total


def middle_kernel(scale, *refs):
    sources, got, outs = refs[:4], refs[4], refs[5:11]
    section, mid, own, a, b, src = outs
    held, strips, lines, sems = refs[11:15], refs[15], refs[16], refs[17]
    meta, pre, q_ref, pick = held
    pairs = [(sources[0], meta), (sources[3], pick)]
    for block in range(2):
        pairs += [(sources[i].at[block], held[i].at[block]) for i in (1, 2)]
    loads = loads_of(pairs, sems)
    start_all(loads[:4])
    inject(got, src, lines)
    start_all(loads[4:])

    def body(block):
        @pl.when(block == 0)
        def _():
            wait_all(loads[:4])

        @pl.when(block == 1)
        def _():
            wait_all(loads[4:])

        for f in range(FIELDS):
            value = pre[block, f]
            line = scale * src[0, block, pl.ds(f, 1), pl.ds(0, PLANE)]
            top = value[:8]
            top = jnp.where(iota((8, PLANE), 0) == 0, top + line, top)
            section[block, f, pl.ds(0, 8), :] = top
            section[block, f, pl.ds(8, W - 8), :] = value[8:]
            mid[block, f, pl.ds(0, 8), :] = q_ref[block, f, pl.ds(0, 8), :] + top
            mid[block, f, pl.ds(8, W - 8), :] = q_ref[block, f, pl.ds(8, W - 8), :] + value[8:]
        extract(mid, block, pick, own, strips)

    both_blocks(body)
    hand_out(own, a, b, meta)


def early_kernel(meta, link, kind, own, a, faces, swapped):
    for face in range(12):
        source = meta[0, face]

        @pl.when(source < 12 + FACE_CAP)
        def _():
            keep = jnp.where(kind[face // 6, face % 6] == 2, 0.0, 1.0).astype(F32)
            code = link[2, face // 6, face % 6]
            turn_face(own, a, None, source, code, keep, faces, face, swapped.at[face % 6])


def interior_kernel(scale, x_ref, section, vel, th, me, ty, tz, part, out_hbm, d_ref, sem):
    copy = pltpu.make_async_copy(section, out_hbm, sem)
    copy.start()

    def body(block):
        def emit(f, g, rows, lanes, w, value):
            part[block, f, rows, lanes] = -value

        sweep(block, scale, x_ref, (ty, tz), None, (vel, th, me), d_ref, emit)

    both_blocks(body)
    copy.wait()


def ghost_kernel(scale, last, *refs):
    meta, link, kind = refs[:3]
    own, a, b = (None, None, refs[4]) if last else refs[3:6]
    early = refs[3] if last else None
    refs = refs[5 if last else 6 :]
    part, vel, th, me, zg = refs[:5]
    src = refs[5] if last else None
    refs = refs[5 + last :]
    out_hbm, ghost, d_ref, out, sems = refs[0], refs[1:6], refs[6], refs[7], refs[8]

    def copy(block):
        return pltpu.make_async_copy(out.at[block], out_hbm.at[block], sems.at[block])

    def body(block):
        prepare_ghosts(block, meta, link, kind, own, a, b, ghost, early)

        def emit(f, g, rows, lanes, w, value):
            value = part[block, f, rows, lanes] - value
            if last and g == 0:
                line = scale * src[1, block, pl.ds(f, 1), lanes]
                value = jnp.where(iota((8, w), 0) == 0, value + line, value)
            out[block, f, rows, lanes] = value

        sweep(block, scale, None, None, tuple(ghost) + (zg,), (vel, th, me), d_ref, emit)
        copy(block).start()

    both_blocks(body)
    for block in range(2):
        copy(block).wait()


SMEM = pl.BlockSpec(memory_space=pltpu.SMEM)
VMEM = pl.BlockSpec(memory_space=pltpu.VMEM)
ANY = pl.BlockSpec(memory_space=pl.ANY)


def near(x):
    return pltpu.with_memory_space_constraint(x, pltpu.VMEM)


def far(x):
    return pltpu.with_memory_space_constraint(x, pltpu.HBM)


def cost(flops, size):
    return pl.CostEstimate(flops=flops, bytes_accessed=size, transcendentals=0)


def call(kernel, name, arrays, outs, scratch, flops=0, size=10**6, smem=(), remote=()):
    specs = [VMEM if spot is None else spot for spot, _ in outs]
    return pl.pallas_call(
        kernel,
        in_specs=[SMEM] * len(smem) + [ANY] * len(remote) + [VMEM] * len(arrays),
        out_specs=specs,
        out_shape=[shape for _, shape in outs],
        scratch_shapes=scratch,
        compiler_params=pltpu.CompilerParams(vmem_limit_bytes=VMEM_LIMIT),
        cost_estimate=cost(flops, size),
        name=name,
    )(*smem, *[far(x) for x in remote], *[near(x) for x in arrays])


def held_in(x, kind=pltpu.VMEM):
    return kind(x.shape, x.dtype)


def out_far(shape, dtype=F32):
    return (ANY, pltpu.HBM(shape, dtype))


def out_near(shape):
    return (None, pltpu.VMEM(shape, F32))


VOLUME = (2, FIELDS, W, PLANE)
FACE = (ROWS, 128)


def exchange(a, b):
    n = lax.axis_size("blk")
    odd = [(i, (i + 1) % n) for i in range(1, n, 2)]
    b = lax.ppermute(b, "blk", odd + [(j, i) for i, j in odd])
    return lax.ppermute(a, "blk", [(i, i ^ 1) for i in range(n)]), b


def local(field, velocity, thermo, metric, inlet_rows, row_owner, face_link, face_kind):
    devices = lax.axis_size("les") * lax.axis_size("blk")
    ty = jnp.asarray(second_table(), BF16)
    tz = jnp.asarray(third_tables(), BF16)
    zg = jnp.asarray(third_ghost_table(), BF16)
    pick = jnp.asarray(third_pick_table(), BF16)
    c1, c2 = (TIME_STEP * w for w in SECTION_WEIGHTS)
    link = jnp.transpose(face_link, (2, 0, 1))
    means = [velocity, thermo, metric]
    d_scratch = pltpu.VMEM((2, 2, ROWS, 256), F32)
    strips = pltpu.VMEM((W * W, 128), F32)
    volume = pltpu.VMEM(VOLUME, F32)
    counts = [12, FACE_CAP, FACE_CAP]
    dma = pltpu.SemaphoreType.DMA

    inputs = [row_owner, inlet_rows, link, face_kind, field, pick]
    sent, own, a, b, meta = call(
        first_kernel,
        "first_faces",
        [],
        [out_far((devices, 8, 128))]
        + [out_far((n,) + FACE) for n in counts]
        + [out_far((2, 12), jnp.int32)],
        [
            held_in(row_owner, pltpu.SMEM),
            pltpu.SMEM((devices,), jnp.int32),
            held_in(link, pltpu.SMEM),
            held_in(face_kind, pltpu.SMEM),
            pltpu.SMEM((2, 12), jnp.int32),
            held_in(inlet_rows),
            pltpu.VMEM((4, inlet_rows.shape[1], 128), F32),
            pltpu.VMEM((devices, 8, 128), F32),
            volume,
            held_in(pick),
            pltpu.VMEM((12,) + FACE, F32),
            strips,
            dma((9,)),
            dma((2,)),
            dma((12,)),
        ],
        10**9,
        remote=inputs,
    )
    a, b = exchange(a, b)
    got = lax.all_to_all(sent, ("les", "blk"), split_axis=0, concat_axis=0, tiled=True)
    scalars = [meta, link, face_kind]
    ghost_scratch = GHOST_SCRATCH + [d_scratch, volume, dma((2,))]
    part, *means = call(
        functools.partial(inner_kernel, c1),
        "inner_first",
        [],
        [out_near(x.shape) for x in [field] + means],
        [held_in(ty), held_in(tz), volume, d_scratch, dma((10,))],
        100000000,
        1000000,
        remote=[ty, tz, field] + means,
    )
    (pre,) = call(
        functools.partial(ghost_kernel, c1, False),
        "ghosts_first",
        [own, a, b, part] + means + [zg],
        [out_far(VOLUME)],
        ghost_scratch,
        2000000000,
        1000000,
        smem=scalars,
    )
    got = got.reshape(devices * 8, 128)
    inputs = [meta, pre, field, pick]
    section, middle, own, a, b, src = call(
        functools.partial(middle_kernel, c1),
        "middle_faces",
        [got],
        [out_near(VOLUME), out_near(VOLUME)]
        + [out_near((n,) + FACE) for n in counts]
        + [out_near((2, 2, 8, 128 * TILES))],
        [held_in(meta, pltpu.SMEM)]
        + [held_in(x) for x in inputs[1:]]
        + [strips, pltpu.VMEM((W * 8, 128), F32), dma((6,))],
        2 * 10**9,
        6 * 10**6,
        remote=inputs,
    )
    means = [velocity, thermo, metric]
    a, b = exchange(a, b)
    part, first = call(
        functools.partial(interior_kernel, c2),
        "interior",
        [middle, section] + means + [ty, tz],
        [out_near(VOLUME), out_far(VOLUME)],
        [d_scratch, dma],
        6 * 10**9,
        12 * 10**6,
    )
    (early,) = call(
        early_kernel,
        "turn_early",
        [own, a],
        [out_near((12,) + FACE)],
        [pltpu.VMEM((6,) + FACE, F32)],
        10**8,
        10**6,
        smem=scalars,
    )
    (second,) = call(
        functools.partial(ghost_kernel, c2, True),
        "ghosts_last",
        [early, b, part] + means + [zg, src],
        [out_far(VOLUME)],
        ghost_scratch,
        2 * 10**9,
        smem=scalars,
    )
    return first, second


def solution(mesh):
    both = ("les", "blk")
    return jax.shard_map(
        local,
        mesh=mesh,
        in_specs=(
            P(both, None, None, None),
            P(both, None, None, None),
            P(both, None, None, None),
            P(both, None, None, None),
            P(None, both, None),
            P(both),
            P(both, None, None),
            P(both, None),
        ),
        out_specs=(P(both, None, None, None), P(both, None, None, None)),
        check_vma=False,
    )
```
